512 devices in a mesh: mp: 4 (over z_hi), space: 128 (over x, z_lo, y, core).
Axes of the slice: x: 4, y: 4, z: 16 (z_hi: 4, z_lo: 4; z = z_hi * 4 + z_lo), core: 2. Of those that a mesh axis runs over, the one named last changes fastest.
Arguments:
- density: float32 [4, 8192, 128], P('mp', 'space'), may hold values from 0.5 to 2
- fields: float32 [4, 7, 8192, 128], P('mp', None, 'space'), may hold values from -3 to 3
- src_points: int32 [4, 128, 128, 64], P('mp', 'space'), may hold values from 0 to 8191
- dst_points: int32 [4, 128, 128, 64], P('mp', 'space'), may hold values from 0 to 8191, as said below
- recv_count: int32 [4, 128, 128], P('mp', 'space'), may hold values from 16 to 64, as said below
- iono_owner: int32 [16384], replicated, may hold values from 0 to 255, as said below
- iono_cell: int32 [16384], replicated, may hold values from 0 to 8191
- response: bfloat16 [16384, 16384], P(('mp', 'space')), may hold values from -0.046875 to 0.046875
Outputs:
- density_out: float32 [4, 8192, 128], P('mp', 'space')
- fields_out: float32 [4, 7, 8192, 128], P('mp', None, 'space')
The draws below stay inside these ranges and needn't reach their ends.
Inputs may be any that keep to these rules, and one draw needn't show every extreme that they name: Within one block of the receiving section the cells dst_points[s, k, :, :] are all different. `recv_count`: in every section one block receives all 64 slots from every block of the section before it. `iono_owner`: magnetosphere blocks are numbered (section - 2) * 128 + block; no two ionosphere points share both owner and cell.
All inputs are finite; a program needn't handle non-finite values.
Results may differ from the reference program's by a relative error of at most 0.0003.
Values sent between devices are 32-bit elements; how exact they have to be, the bound alone decides.
A program may use at most 64 MiB of HBM per device.

```python
import math
import jax
import jax.numpy as jnp
from jax import lax

COMPONENTS = 8
FIELD_COMPONENTS = 7
BLOCK_ROWS = 64
BLOCK_COLS = 128
BLOCK_CELLS = 8192
ROWS_ALL = 8192
POINTS = 64
TIME_STEPS = 2
IONO_GRID = 16384
N_MP = 4
N_SPACE = 128


def shared_cells(key):
    return jax.random.permutation(key, 2 * N_SPACE * BLOCK_ROWS * BLOCK_COLS)[:IONO_GRID]


def draw_dst_points(key, part):
    key = jax.random.fold_in(key, 11)
    many_keys = jax.random.split(key, N_MP * N_SPACE)

    def pick_cells(one_key):
        return jax.random.permutation(one_key, BLOCK_ROWS * BLOCK_COLS)[:N_SPACE * POINTS]
    chosen = jax.vmap(pick_cells)(many_keys)
    return chosen.reshape(N_MP, N_SPACE, N_SPACE, POINTS).astype(jnp.int32)


def draw_recv_count(key, part):
    key = jax.random.fold_in(key, 23)
    first_key, second_key = jax.random.split(key)
    counted = jax.random.randint(first_key, (N_MP, N_SPACE, N_SPACE), POINTS // 4, POINTS + 1)
    full_target = jax.random.randint(second_key, (N_MP, 1, 1), 0, N_SPACE)
    target_index = jnp.arange(N_SPACE).reshape(1, N_SPACE, 1)
    return jnp.where(target_index == full_target, POINTS, counted).astype(jnp.int32)


def draw_iono_owner(key, part):
    picked = shared_cells(key)
    return (picked // (BLOCK_ROWS * BLOCK_COLS)).astype(jnp.int32)


def draw_iono_cell(key, part):
    picked = shared_cells(key)
    return (picked % (BLOCK_ROWS * BLOCK_COLS)).astype(jnp.int32)


def touch_ends(array, rng, smallest, largest):
    dims = array.shape
    index_at = [jax.random.randint(jax.random.fold_in(rng, axis), (), 0, dims[axis]) for axis in range(len(dims))]
    array = array.at[tuple(index_at)].set(smallest)
    longest = dims.index(max(dims))
    index_at[longest] = (index_at[longest] + 1) % dims[longest]
    return array.at[tuple(index_at)].set(largest)


def level_of(stream_key, extent, cuts, low, largest):
    level = 1.0
    for axis_at, blocks in cuts:
        heights = jax.random.uniform(jax.random.fold_in(jax.random.fold_in(stream_key, 6), axis_at), (blocks,), jnp.float32, low / len(cuts), largest / len(cuts))
        level = level * jnp.repeat(jnp.exp(heights), extent[axis_at] // blocks).reshape((-1,) + (1,) * (len(extent) - 1 - axis_at))
    return level


def normal_values(own_key, shape, deviation, most, cuts=(), held_as=jnp.bfloat16):
    gain = level_of(own_key, shape, cuts, -0.22, 0.18) if cuts else 1.0
    result = jax.random.normal(own_key, shape, jnp.float32) * deviation * gain
    return jnp.minimum(jnp.maximum(result, -most), most).astype(held_as)


def setup_inputs(seed: int = 0) -> dict:
    streams_of = jax.random.split(jax.random.key(seed), 9)
    return {
        "density": jnp.clip(jnp.exp(math.log(2.0) - 1.3862944 * jax.random.uniform(streams_of[0], (N_MP, ROWS_ALL, BLOCK_COLS), jnp.float32) ** level_of(streams_of[0], (N_MP, ROWS_ALL, BLOCK_COLS), ((0, 4), (1, 128)), -0.2, 0.2)), 0.5, 2.0),
        "fields": normal_values(streams_of[1], (N_MP, FIELD_COMPONENTS, ROWS_ALL, BLOCK_COLS), 0.5, 3.0, ((0, 4), (2, 128)), jnp.float32),
        "src_points": touch_ends(jax.random.randint(streams_of[2], (N_MP, N_SPACE, N_SPACE, POINTS), 0, BLOCK_CELLS), jax.random.fold_in(streams_of[2], 1), 0, BLOCK_CELLS - 1).astype(jnp.int32),
        "dst_points": draw_dst_points(jax.random.fold_in(streams_of[8], 71), 0),
        "recv_count": draw_recv_count(jax.random.fold_in(streams_of[8], 71), 0),
        "iono_owner": draw_iono_owner(jax.random.fold_in(streams_of[8], 71), 0),
        "iono_cell": draw_iono_cell(jax.random.fold_in(streams_of[8], 71), 0),
        "response": normal_values(streams_of[7], (IONO_GRID, IONO_GRID), IONO_GRID ** -0.5, 0.046875, ((0, 512),)),
    }


LAMBDA_STEP = 0.1
SOUND_SPEED = 1.0


def slice_span(array_in, start_at, trim_end, axis_dim):
    return lax.slice_in_dim(array_in, start_at, array_in.shape[axis_dim] - trim_end, axis=axis_dim)


def advance(padded, speed_row, axis_dim):
    velocity = padded[speed_row] / padded[0]
    flux_all = padded * velocity[None]
    lower_speed = jnp.abs(slice_span(velocity, 0, 1, axis_dim - 1))
    upper_speed = jnp.abs(slice_span(velocity, 1, 0, axis_dim - 1))
    signal_speed = jnp.maximum(lower_speed, upper_speed) + SOUND_SPEED
    face_flux = 0.5 * (slice_span(flux_all, 0, 1, axis_dim) + slice_span(flux_all, 1, 0, axis_dim)) - 0.5 * signal_speed[None] * (slice_span(padded, 1, 0, axis_dim) - slice_span(padded, 0, 1, axis_dim))
    return slice_span(padded, 1, 1, axis_dim) - LAMBDA_STEP * (slice_span(face_flux, 1, 0, axis_dim) - slice_span(face_flux, 0, 1, axis_dim))


def column_sweep(section_state):
    padded = jnp.concatenate([section_state[:, :, :1], section_state, section_state[:, :, -1:]], axis=2)
    return advance(padded, 1, 2)


def sweep_section(section_state):
    for substep in range(TIME_STEPS):
        section_state = column_sweep(section_state)
        padded = jnp.concatenate([section_state[:, -1:], section_state, section_state[:, :1]], axis=1)
        section_state = advance(padded, 2, 1)
    return section_state


def pack_block(block, chosen):
    return block[:, chosen.reshape(-1)]


def place_block(block, arrived, targets, counted):
    block_cells = block.shape[1]
    usable = jnp.arange(targets.shape[1])[None, :] < counted[:, None]
    target = jnp.where(usable, targets, block_cells).reshape(-1)
    return block.at[:, target].set(arrived, mode="drop")


def reference(density, fields, src_points, dst_points, recv_count, iono_owner, iono_cell, response):
    block_cells = BLOCK_ROWS * BLOCK_COLS
    plasma_state = jnp.concatenate([density[:, None], fields], axis=1)
    blocks_start = plasma_state.reshape(N_MP, COMPONENTS, N_SPACE, block_cells)
    outgoing = jax.vmap(jax.vmap(pack_block, in_axes=(1, 0)), in_axes=(0, 0))(blocks_start, src_points)
    outgoing = outgoing.reshape(N_MP, N_SPACE, COMPONENTS, N_SPACE, POINTS)
    incoming = jnp.transpose(outgoing, (0, 3, 2, 1, 4)).reshape(N_MP, N_SPACE, COMPONENTS, N_SPACE * POINTS)
    magnetic = plasma_state[:, 6]
    edges = jnp.concatenate([magnetic[:, :, :1], magnetic, magnetic[:, :, -1:]], axis=2)
    current_all = (0.5 * (edges[:, :, 2:] - edges[:, :, :-2])).reshape(N_MP, N_SPACE, block_cells)
    current_mag = current_all[2:].reshape(2 * N_SPACE, block_cells)
    iono_current = current_mag[iono_owner, iono_cell]
    potential = jnp.dot(response.astype(jnp.float32), iono_current, precision=lax.Precision.HIGHEST, preferred_element_type=jnp.float32)
    sections_out = [sweep_section(plasma_state[0]).reshape(COMPONENTS, N_SPACE, block_cells)]
    for section in range(1, N_MP):
        blocks = sweep_section(plasma_state[section]).reshape(COMPONENTS, N_SPACE, block_cells)
        placed = jax.vmap(place_block, in_axes=(1, 0, 0, 0), out_axes=1)(blocks, incoming[section - 1], dst_points[section], recv_count[section])
        sections_out.append(placed)
    combined = jnp.stack(sections_out)
    magneto = jnp.transpose(combined[2:], (1, 0, 2, 3)).reshape(COMPONENTS, 2 * N_SPACE, block_cells)
    drift_push = 0.5 * magneto[0, iono_owner, iono_cell] * potential
    momentum = magneto[1].at[iono_owner, iono_cell].add(drift_push)
    magneto = magneto.at[1].set(momentum)
    magneto = jnp.transpose(magneto.reshape(COMPONENTS, 2, N_SPACE, block_cells), (1, 0, 2, 3))
    combined = jnp.concatenate([combined[:2], magneto], axis=0)
    combined = combined.reshape(N_MP, COMPONENTS, ROWS_ALL, BLOCK_COLS)
    return combined[:, 0], combined[:, 1:]
```

```python
import functools

import jax
import jax.numpy as jnp
from jax import lax
from jax.experimental import pallas as pl
from jax.experimental.pallas import tpu as pltpu
from jax.sharding import PartitionSpec as P

MESH = pl.DeviceIdType.MESH
YC = 8
XZ = 16
LAMBDA_STEP = 0.1
F32 = jnp.float32
I32 = jnp.int32
BF16 = jnp.bfloat16


def iota(shape, dim):
    return lax.broadcasted_iota(I32, shape, dim)


def pick(tables, count, row, lane):
    shape = row.shape

    def step(r, held):
        hit = row == r
        return tuple(
            jnp.where(
                hit,
                jnp.take_along_axis(jnp.broadcast_to(line, shape), lane, axis=1, mode="promise_in_bounds"),
                old,
            )
            for line, old in zip(tables(r), held)
        )

    start = tuple(jnp.zeros(shape, F32) for _ in tables(0))
    return lax.fori_loop(0, count, step, start, unroll=4)


def pack_kernel(density, fields, src, owner, cell, outbox, contribution, state, index, current):
    mp = lax.axis_index("mp")
    me = (mp - 2) * (XZ * YC) + lax.axis_index("space")
    low = iota((8, 128), 1) < 64
    state[0] = density[0]
    for c in range(7):
        state[c + 1] = fields[0, c]

    @pl.when(mp >= 2)
    def _():
        b = state[6]
        col = iota((64, 128), 1)
        right = jnp.where(col == 127, b, pltpu.roll(b, 127, 1))
        left = jnp.where(col == 0, b, pltpu.roll(b, 1, 1))
        current[...] = 0.5 * (right - left)
        for half in range(2):
            part = pl.ds(half * 64, 64)
            cells = cell[part, :]
            (got,) = pick(lambda r: (current[pl.ds(r, 1), :],), 64, cells >> 7, cells & 127)
            contribution[part, :] = jnp.where(owner[part, :] == me, got, 0.0)

    @pl.when(mp < 3)
    def _():
        points = src[...]
        turned = jnp.concatenate([points, points], axis=0).T
        index[...] = jnp.where(iota((64, 128), 1) < 64, turned[:64], turned[64:])

        def block(b, carry):
            cells = index[pl.ds(b * 16, 16), :]
            got = pick(lambda r: tuple(state[c, pl.ds(r, 1), :] for c in range(8)), 64, cells >> 7, cells & 127)
            for half in range(2):
                for q in range(4):
                    first = got[2 * q][half * 8 : half * 8 + 8]
                    second = got[2 * q + 1][half * 8 : half * 8 + 8]
                    xz = b * 2 + half
                    outbox[pl.ds(xz * 4 + q, 8, stride=64), :] = jnp.where(low, first, pltpu.roll(second, 64, 1))
                    outbox[pl.ds((xz + 8) * 4 + q, 8, stride=64), :] = jnp.where(low, pltpu.roll(first, 64, 1), second)
            return carry

        lax.fori_loop(0, 4, block, 0)


def invert(rows_ref, used, high_of, low_of, count):
    def step(b, total):
        cells = rows_ref[pl.ds(b * 8, 8), :]
        keep = used(b)
        row8 = jnp.where(keep, cells >> 7, -1)
        col8 = cells & 127
        left, right = [], []
        for s in range(8):
            hit = iota((64, 128), 0) == row8[s : s + 1]
            left.append(
                jnp.concatenate(
                    [jnp.where(hit, high_of(b * 8 + s), 0.0), jnp.where(hit, low_of(b * 8 + s), 0.0)], axis=0
                ).astype(BF16)
            )
            right.append(jnp.where(iota((128, 128), 0) == col8[s : s + 1], 1.0, 0.0).astype(BF16))
        return total + lax.dot_general(
            jnp.concatenate(left, axis=1),
            jnp.concatenate(right, axis=1),
            (((1,), (1,)), ((), ())),
            preferred_element_type=F32,
        )

    return lax.fori_loop(0, count // 8, step, jnp.zeros((128, 128), F32))


def sweep(work, speed, axis):
    shape = (80, 128)
    size = shape[axis]
    at = iota(shape, axis)

    def above(value):
        moved = pltpu.roll(value, size - 1, axis)
        return jnp.where(at == size - 1, value, moved) if axis == 1 else moved

    u = work[speed] / work[0]
    u_up = above(u)
    fast = 0.5 * (jnp.maximum(jnp.abs(u), jnp.abs(u_up)) + 1.0)
    for c in range(8):
        q = work[c]
        flux = u * q
        face = 0.5 * (flux + above(flux)) - fast * (above(q) - q)
        below = pltpu.roll(face, 1, axis)
        if axis == 1:
            below = jnp.where(at == 0, flux, below)
        work[c] = q - LAMBDA_STEP * (face - below)


def wait_for(ref, sem):
    pltpu.make_async_copy(ref, ref, sem).wait()


def exchange_kernel(
    density, fields, dst, recv_count, owner, cell, response, outbox, contribution,
    swept, inbox_out, potential, slot_code, iono_code,
    work, halo_out, halo_in, mid, inbox, rs, part, ar, full, spread, line, lines, tile, pot_part, pot,
    halo_send, halo_recv, send, rs_recv, ar_recv, full_recv, mid_recv, inbox_recv, line_recv, pot_recv,
):
    mp = lax.axis_index("mp")
    space = lax.axis_index("space")
    xz = lax.div(space, YC)
    yc = lax.rem(space, YC)
    magnetic = mp >= 2
    a_me = mp * YC + yc
    size = XZ * YC

    def a_device(a):
        return (lax.div(a, YC), xz * YC + lax.rem(a, YC))

    def b_device(x):
        return (mp, x * YC + yc)

    def loop(first, last, body):
        def step(i, carry):
            body(i)
            return carry

        lax.fori_loop(first, last, step, 0)

    barrier = pltpu.get_barrier_semaphore()

    def greet(device):
        pl.semaphore_signal(barrier, inc=1, device_id=device, device_id_type=MESH)

    after = (mp, lax.rem(space + 1, size))
    before = (mp, lax.rem(space + size - 1, size))
    greet(after)
    greet(before)
    loop(1, XZ, lambda i: greet(b_device(lax.rem(xz + i, XZ))))
    loop(1, 4 * YC, lambda i: greet(a_device(lax.rem(a_me + i, 4 * YC))))

    work[...] = jnp.ones_like(work)
    work[0, 8:72, :] = density[0]
    for c in range(7):
        work[c + 1, 8:72, :] = fields[0, c]
    for c in range(8):
        for i in range(2):
            halo_out[0, pl.ds(i * 8 + c, 1), :] = work[c, 8 + i : 9 + i, :]
            halo_out[1, pl.ds(i * 8 + c, 1), :] = work[c, 70 + i : 71 + i, :]

    pl.semaphore_wait(barrier, 2 + XZ - 1 + 4 * YC - 1)

    def push(src_ref, dst_ref, send_sem, recv_sem, device):
        pltpu.make_async_remote_copy(
            src_ref=src_ref, dst_ref=dst_ref, send_sem=send_sem, recv_sem=recv_sem,
            device_id=device, device_id_type=MESH,
        ).start()

    @pl.when(magnetic)
    def _():
        def one(i):
            to = lax.rem(xz + i, XZ)
            push(contribution.at[to], rs.at[xz], send.at[0], rs_recv, b_device(to))

        loop(1, XZ, one)
        rs[xz] = contribution[xz]

    push(halo_out.at[0], halo_in.at[1], halo_send.at[0], halo_recv.at[1], before)
    push(halo_out.at[1], halo_in.at[0], halo_send.at[1], halo_recv.at[0], after)

    @pl.when(mp < 3)
    def _():
        def one(i):
            to = lax.rem(yc + i, YC)
            push(outbox.at[to], mid.at[yc], send.at[1], mid_recv, (mp + 1, xz * YC + to))

        loop(0, YC, one)

    @pl.when(magnetic)
    def _():
        wait_for(rs.at[pl.ds(0, XZ - 1)], rs_recv)
        total = rs[0]
        for i in range(1, XZ):
            total = total + rs[i]
        part[...] = total
        mine = a_me - 2 * YC

        def one(i):
            push(part, ar.at[mine], send.at[2], ar_recv, a_device(lax.rem(a_me + i, 4 * YC)))

        loop(1, 4 * YC, one)
        ar[mine] = total

    lane = iota((1, 128), 1)

    @pl.when(mp > 0)
    def _():
        counts = recv_count[...]
        high = ((lane & 63) + 1).astype(F32)

        def used(b):
            return (iota((8, 128), 0) + b * 8) < counts

        def low(p):
            return ((lane >> 6) * 64 + p).astype(F32)

        slot_code[...] = invert(dst, used, lambda p: high, low, 64).astype(I32)

    wait_for(halo_in.at[0], halo_recv.at[0])
    wait_for(halo_in.at[1], halo_recv.at[1])
    for c in range(8):
        for i in range(2):
            work[c, 6 + i : 7 + i, :] = halo_in[0, pl.ds(i * 8 + c, 1), :]
            work[c, 72 + i : 73 + i, :] = halo_in[1, pl.ds(i * 8 + c, 1), :]

    @pl.when(magnetic)
    def _():
        wait_for(ar.at[pl.ds(0, 2 * YC - 1)], ar_recv)

    @pl.when(mp < 2)
    def _():
        wait_for(ar.at[pl.ds(0, 2 * YC)], ar_recv)

    total = ar[0]
    for i in range(1, 2 * YC):
        total = total + ar[i]
    full[...] = total

    def give(i):
        push(full, spread.at[xz], send.at[3], full_recv, b_device(lax.rem(xz + i, XZ)))

    loop(1, XZ, give)
    spread[xz] = total

    for _ in range(2):
        sweep(work, 1, 1)
        sweep(work, 2, 0)
    swept[...] = work[:, 8:72, :]

    wait_for(spread.at[pl.ds(0, XZ - 1)], full_recv)
    acc = jnp.zeros((32, 128), F32)
    for i in range(128):
        acc = acc + response[:, i * 128 : (i + 1) * 128].astype(F32) * spread[i // 8, i % 8 : i % 8 + 1, :]
    tile[...] = jnp.zeros_like(tile)
    tile[pl.ds(pl.multiple_of(lax.rem(yc, 4) * 32, 32), 32), :] = acc
    line[...] = jnp.sum(tile[...].T, axis=0, keepdims=True)

    @pl.when(magnetic)
    def _():
        mine = a_me - 2 * YC

        def one(i):
            to = lax.rem(mine + i, 2 * YC)
            push(line, lines.at[a_me], send.at[4], line_recv, a_device(to + 2 * YC))

        loop(1, 2 * YC, one)
        lines[a_me] = line[...]

    @pl.when(mp < 2)
    def _():
        def one(i):
            to = lax.rem(yc + i, 2 * YC)
            push(line, lines.at[a_me], send.at[4], line_recv, a_device(to + 2 * YC))

        loop(0, 2 * YC, one)

    @pl.when(mp > 0)
    def _():
        wait_for(mid, mid_recv)

        def one(i):
            to = lax.rem(xz + i, XZ)
            push(mid.at[:, to], inbox.at[xz], send.at[5], inbox_recv, b_device(to))

        loop(1, XZ, one)
        inbox[xz] = mid[:, xz]

    @pl.when(magnetic)
    def _():
        me = (mp - 2) * size + space

        def used(b):
            return owner[pl.ds(b * 8, 8), :] == me

        def high(i):
            return ((lax.rem(lax.div(i, 2), 16) * 8 + lax.div(i, 32) * 2 + lax.rem(i, 2)) + 1).astype(F32)

        low = lane.astype(F32)
        iono_code[...] = invert(cell, used, high, lambda i: low, 128).astype(I32)

        wait_for(lines.at[pl.ds(0, 4 * YC - 1)], line_recv)
        rows = []
        for m in range(4):
            for h in range(2):
                row = lines[m * 8 + h * 4]
                for i in range(1, 4):
                    row = row + lines[m * 8 + h * 4 + i]
                rows.append(row)
        mine = jnp.concatenate(rows, axis=0)
        pot_part[...] = mine

        def one(i):
            push(pot_part, pot.at[xz], send.at[6], pot_recv, b_device(lax.rem(xz + i, XZ)))

        loop(1, XZ, one)
        pot[xz] = mine
        wait_for(pot.at[pl.ds(0, XZ - 1)], pot_recv)
        potential[...] = pot[...]

    @pl.when(mp > 0)
    def _():
        wait_for(inbox.at[pl.ds(0, XZ - 1)], inbox_recv)
        inbox_out[...] = inbox[...]

    wait_for(halo_out.at[0], halo_send.at[0])
    wait_for(halo_out.at[1], halo_send.at[1])
    wait_for(spread.at[pl.ds(0, XZ - 1)], send.at[3])

    @pl.when(mp < 3)
    def _():
        wait_for(mid, send.at[1])

    @pl.when(mp > 0)
    def _():
        wait_for(inbox.at[pl.ds(0, XZ - 1)], send.at[5])

    @pl.when(magnetic)
    def _():
        wait_for(rs.at[pl.ds(0, XZ - 1)], send.at[0])
        wait_for(ar.at[pl.ds(0, 4 * YC - 1)], send.at[2])
        wait_for(lines.at[pl.ds(0, 2 * YC - 1)], send.at[4])
        wait_for(pot.at[pl.ds(0, XZ - 1)], send.at[6])

    @pl.when(mp < 2)
    def _():
        wait_for(lines.at[pl.ds(0, 2 * YC)], send.at[4])


def place_kernel(swept, inbox, potential, slot_code, iono_code, density_out, fields_out, state, table):
    mp = lax.axis_index("mp")
    low = iota((8, 128), 1) < 64

    @pl.when(mp == 0)
    def _():
        state[...] = swept[...]

    @pl.when(mp > 0)
    def _():
        for b in range(8):
            for q in range(4):
                first = inbox[pl.ds(b * 32 + q, 8, stride=4), :]
                second = inbox[pl.ds((b + 8) * 32 + q, 8, stride=4), :]
                table[2 * q, b * 8 : b * 8 + 8, :] = jnp.where(low, first, pltpu.roll(second, 64, 1))
                table[2 * q + 1, b * 8 : b * 8 + 8, :] = jnp.where(low, pltpu.roll(first, 64, 1), second)

        def block(b, carry):
            part = pl.ds(b * 16, 16)
            row = slot_code[part, :] - 1
            lane = slot_code[pl.ds(64 + b * 16, 16), :]
            got = pick(lambda r: tuple(table[c, pl.ds(r, 1), :] for c in range(8)), 64, row, lane)
            for c in range(8):
                state[c, part, :] = jnp.where(row >= 0, got[c], swept[c, part, :])
            return carry

        lax.fori_loop(0, 4, block, 0)

    @pl.when(mp >= 2)
    def _():
        row = iono_code[:64, :] - 1
        lane = iono_code[64:, :]
        (got,) = pick(lambda r: (potential[pl.ds(r, 1), :],), 128, row, lane)
        state[1] = state[1] + jnp.where(row >= 0, 0.5 * state[0] * got, 0.0)

    density_out[0] = state[0]
    for c in range(7):
        fields_out[0, c] = state[c + 1]


VMEM = pl.BlockSpec(memory_space=pltpu.VMEM)


def local(density, fields, src_points, dst_points, recv_count, iono_owner, iono_cell, response):
    src = src_points[0, 0].T
    dst = dst_points[0, 0].T
    owner = iono_owner.reshape(128, 128)
    cell = iono_cell.reshape(128, 128)
    outbox, contribution = pl.pallas_call(
        pack_kernel,
        out_shape=[jax.ShapeDtypeStruct((512, 128), F32), jax.ShapeDtypeStruct((128, 128), F32)],
        in_specs=[VMEM] * 5,
        out_specs=[VMEM] * 2,
        scratch_shapes=[
            pltpu.VMEM((8, 64, 128), F32),
            pltpu.VMEM((64, 128), I32),
            pltpu.VMEM((64, 128), F32),
        ],
        compiler_params=pltpu.CompilerParams(vmem_limit_bytes=24 * 1024 * 1024),
        name="pack",
    )(density, fields, src, owner, cell)
    dma = pltpu.SemaphoreType.DMA
    swept, inbox, potential, slot_code, iono_code = pl.pallas_call(
        exchange_kernel,
        out_shape=[
            jax.ShapeDtypeStruct((8, 64, 128), F32),
            jax.ShapeDtypeStruct((XZ, YC, 4, 128), F32),
            jax.ShapeDtypeStruct((XZ, 8, 128), F32),
            jax.ShapeDtypeStruct((128, 128), I32),
            jax.ShapeDtypeStruct((128, 128), I32),
        ],
        in_specs=[VMEM] * 9,
        out_specs=[VMEM] * 5,
        scratch_shapes=[
            pltpu.VMEM((8, 80, 128), F32),
            pltpu.VMEM((2, 16, 128), F32),
            pltpu.VMEM((2, 16, 128), F32),
            pltpu.VMEM((YC, XZ, 4, 128), F32),
            pltpu.VMEM((XZ, YC, 4, 128), F32),
            pltpu.VMEM((XZ, 8, 128), F32),
            pltpu.VMEM((8, 128), F32),
            pltpu.VMEM((4 * YC, 8, 128), F32),
            pltpu.VMEM((8, 128), F32),
            pltpu.VMEM((XZ, 8, 128), F32),
            pltpu.VMEM((1, 128), F32),
            pltpu.VMEM((4 * YC, 1, 128), F32),
            pltpu.VMEM((128, 128), F32),
            pltpu.VMEM((8, 128), F32),
            pltpu.VMEM((XZ, 8, 128), F32),
            dma((2,)),
            dma((2,)),
            dma((7,)),
            dma,
            dma,
            dma,
            dma,
            dma,
            dma,
            dma,
        ],
        compiler_params=pltpu.CompilerParams(
            collective_id=0, has_side_effects=True, vmem_limit_bytes=24 * 1024 * 1024
        ),
        name="exchange",
    )(
        density, fields, dst, recv_count[0], owner, cell, response,
        outbox.reshape(YC, XZ, 4, 128), contribution.reshape(XZ, 8, 128),
    )
    return pl.pallas_call(
        place_kernel,
        out_shape=[jax.ShapeDtypeStruct((1, 64, 128), F32), jax.ShapeDtypeStruct((1, 7, 64, 128), F32)],
        in_specs=[VMEM] * 5,
        out_specs=[VMEM] * 2,
        scratch_shapes=[pltpu.VMEM((8, 64, 128), F32), pltpu.VMEM((8, 64, 128), F32)],
        compiler_params=pltpu.CompilerParams(vmem_limit_bytes=24 * 1024 * 1024),
        name="place",
    )(swept, inbox.reshape(512, 128), potential.reshape(128, 128), slot_code, iono_code)


def solution(mesh):
    placed = (
        P("mp", "space", None),
        P("mp", None, "space", None),
        P("mp", "space", None, None),
        P("mp", "space", None, None),
        P("mp", "space", None),
        P(),
        P(),
        P(("mp", "space"), None),
    )
    return jax.shard_map(
        local,
        mesh=mesh,
        in_specs=placed,
        out_specs=(P("mp", "space", None), P("mp", None, "space", None)),
        check_vma=False,
    )
```

```python
import jax
import jax.numpy as jnp
from jax import lax
from jax.experimental import pallas as pl
from jax.experimental.pallas import tpu as pltpu
from jax.sharding import PartitionSpec as P

MESH = pl.DeviceIdType.MESH
YC = 8
ZS = 4
SPACE = 128
PLANE = 32
LEVELS = 16
LAMBDA_STEP = 0.1
F32 = jnp.float32
I32 = jnp.int32
BF16 = jnp.bfloat16


def iota(shape, dim):
    return lax.broadcasted_iota(I32, shape, dim)


def loop(first, last, body):
    def step(i, carry):
        body(i)
        return carry

    lax.fori_loop(first, last, step, 0)


def wait_for(ref, sem):
    pltpu.make_async_copy(ref, ref, sem).wait()


def push(src_ref, dst_ref, send_sem, recv_sem, device):
    pltpu.make_async_remote_copy(
        src_ref=src_ref,
        dst_ref=dst_ref,
        send_sem=send_sem,
        recv_sem=recv_sem,
        device_id=device,
        device_id_type=MESH,
    ).start()


def pick(lines, count, row, lane, held):
    shape = row.shape
    for r in range(count):
        hit = row == r
        held = [
            jnp.where(
                hit,
                jnp.take_along_axis(jnp.broadcast_to(line, shape), lane, axis=1, mode="promise_in_bounds"),
                old,
            )
            for line, old in zip(lines(r), held)
        ]
    return held


def invert(rows_ref, used, high_of, low_of, count):
    def step(b, total):
        cells = rows_ref[pl.ds(b * 8, 8), :]
        row8 = jnp.where(used(b), cells >> 7, -1)
        col8 = cells & 127
        left, right = [], []
        for s in range(8):
            hit = iota((64, 128), 0) == row8[s : s + 1]
            left.append(
                jnp.concatenate(
                    [jnp.where(hit, high_of(b * 8 + s), 0.0), jnp.where(hit, low_of(b * 8 + s), 0.0)], axis=0
                ).astype(BF16)
            )
            right.append(jnp.where(iota((128, 128), 0) == col8[s : s + 1], 1.0, 0.0).astype(BF16))
        return total + lax.dot_general(
            jnp.concatenate(left, axis=1),
            jnp.concatenate(right, axis=1),
            (((1,), (1,)), ((), ())),
            preferred_element_type=F32,
        )

    return lax.fori_loop(0, count // 8, step, jnp.zeros((128, 128), F32))


def sweep(work, speed, axis):
    shape = (80, 128)
    size = shape[axis]
    at = iota(shape, axis)

    def above(value):
        moved = pltpu.roll(value, size - 1, axis)
        return jnp.where(at == size - 1, value, moved) if axis == 1 else moved

    u = work[speed] / work[0]
    u_up = above(u)
    fast = 0.5 * (jnp.maximum(jnp.abs(u), jnp.abs(u_up)) + 1.0)
    for c in range(8):
        q = work[c]
        flux = u * q
        face = 0.5 * (flux + above(flux)) - fast * (above(q) - q)
        below = pltpu.roll(face, 1, axis)
        if axis == 1:
            below = jnp.where(at == 0, flux, below)
        work[c] = q - LAMBDA_STEP * (face - below)


def cycle_kernel(
    density_in, fields_in, src_in, dst_in, count_in, owner_in, cell_in, response_in,
    density_out, fields_out,
    work, src, dst, recv_count, owner, cell, response, index, current, halo_out, halo_in,
    outbox, mid, inbox, table, contribution, rs, part, ar, full, spread, tile, line, lines, pot_part, pot,
    slot_code, iono_code,
    load, halo_send, halo_recv, send, recv, out_send, mid_recv, fwd_send, inbox_recv,
):
    mp = lax.axis_index("mp")
    space = lax.axis_index("space")
    x = lax.div(space, ZS * YC)
    z = lax.rem(lax.div(space, YC), ZS)
    yc = lax.rem(space, YC)
    place = x * YC + yc
    level = mp * ZS + z
    magnetic = mp >= 2
    me = (mp - 2) * SPACE + space

    def in_plane(p):
        return (mp, (lax.div(p, YC) * ZS + z) * YC + lax.rem(p, YC))

    def in_column(l):
        return (lax.div(l, ZS), (x * ZS + lax.rem(l, ZS)) * YC + yc)

    body = pl.ds(8, 64)
    loads = [
        pltpu.make_async_copy(a, b, load.at[i])
        for i, (a, b) in enumerate(
            (
                (fields_in.at[0], work.at[pl.ds(1, 7), body]),
                (density_in.at[0], work.at[0, body]),
                (cell_in, cell),
                (owner_in, owner),
                (src_in, src),
                (dst_in, dst),
                (count_in, recv_count),
                (response_in, response),
            )
        )
    ]
    for copy in loads:
        copy.start()

    barrier = pltpu.get_barrier_semaphore()

    def greet(device):
        pl.semaphore_signal(barrier, inc=1, device_id=device, device_id_type=MESH)

    after = (mp, lax.rem(space + 1, SPACE))
    before = (mp, lax.rem(space + SPACE - 1, SPACE))
    loop(1, LEVELS, lambda i: greet(in_column(lax.rem(level + i, LEVELS))))
    loop(1, PLANE, lambda i: greet(in_plane(lax.rem(place + i, PLANE))))
    greet(after)
    greet(before)

    low = iota((8, 128), 1) < 64
    lane = iota((1, 128), 1)
    for copy in loads[:4]:
        copy.wait()
    for c in range(8):
        work[c, 0:8, :] = jnp.ones((8, 128), F32)
        work[c, 72:80, :] = jnp.ones((8, 128), F32)

    @pl.when(magnetic)
    def _():
        b = work[6, 8:72, :]
        col = iota((64, 128), 1)
        right = jnp.where(col == 127, b, pltpu.roll(b, 127, 1))
        left = jnp.where(col == 0, b, pltpu.roll(b, 1, 1))
        current[...] = 0.5 * (right - left)

        def block(b):
            at = pl.ds(b * 16, 16)
            cells = cell[at, :]
            (got,) = pick(lambda r: (current[r : r + 1, :],), 64, cells >> 7, cells & 127, [jnp.zeros((16, 128), F32)])
            got = jnp.where(owner[at, :] == me, got, 0.0)
            for i in range(4):
                contribution[b * 4 + i] = got[i * 4 : i * 4 + 4]

        loop(0, 8, block)

    for c in range(8):
        for i in range(2):
            halo_out[0, i * 8 + c : i * 8 + c + 1, :] = work[c, 8 + i : 9 + i, :]
            halo_out[1, i * 8 + c : i * 8 + c + 1, :] = work[c, 70 + i : 71 + i, :]
    loads[4].wait()

    @pl.when(mp < 3)
    def _():
        points = src[...]
        turned = jnp.concatenate([points, points], axis=0).T
        index[...] = jnp.where(iota((64, 128), 1) < 64, turned[:64], turned[64:])

    def pack(half):
        def block(b):
            cells = index[pl.ds(half * 32 + b * 16, 16), :]
            got = pick(
                lambda r: tuple(work[c, 8 + r : 9 + r, :] for c in range(8)),
                64, cells >> 7, cells & 127, [jnp.zeros((16, 128), F32)] * 8,
            )
            for i in range(2):
                for q in range(4):
                    first = got[2 * q][i * 8 : i * 8 + 8]
                    second = got[2 * q + 1][i * 8 : i * 8 + 8]
                    outbox[half, b * 2 + i, :, q, :] = jnp.where(low, first, pltpu.roll(second, 64, 1))
                    outbox[half + 2, b * 2 + i, :, q, :] = jnp.where(low, pltpu.roll(first, 64, 1), second)

        loop(0, 2, block)

    def depart(to_x, t):
        def one(i):
            to = lax.rem(z + i, ZS)
            push(outbox.at[to_x, to], mid.at[to_x, z], out_send, mid_recv.at[t], in_column((mp + 1) * ZS + to))

        loop(0, ZS, one)

    halves = (lax.rem(x + 1, 2), lax.rem(x, 2))

    @pl.when(mp < 3)
    def _():
        pack(halves[0])

    pl.semaphore_wait(barrier, LEVELS - 1 + PLANE - 1 + 2)

    @pl.when(magnetic)
    def _():
        def one(i):
            to = lax.rem(place + i, PLANE)
            push(contribution.at[to], rs.at[place], send.at[0], recv.at[0], in_plane(to))

        loop(PLANE // 2, PLANE, one)
        loop(1, PLANE // 2, one)
        rs[place] = contribution[place]

    push(halo_out.at[0], halo_in.at[1], halo_send.at[0], halo_recv.at[1], before)
    push(halo_out.at[1], halo_in.at[0], halo_send.at[1], halo_recv.at[0], after)

    @pl.when(mp < 3)
    def _():
        depart(halves[0], 0)
        depart(halves[0] + 2, 0)
        pack(halves[1])
        depart(lax.rem(x + 2, 4), 1)
        depart(x, 1)

    @pl.when(magnetic)
    def _():
        wait_for(rs.at[pl.ds(0, PLANE - 1)], recv.at[0])
        total = rs[0]
        for i in range(1, PLANE):
            total = total + rs[i]
        part[...] = total

        def one(i):
            push(part, ar.at[level - 8], send.at[1], recv.at[1], in_column(lax.rem(level + i, LEVELS)))

        loop(8, LEVELS, one)
        loop(1, 8, one)
        ar[level - 8] = total

    loads[5].wait()
    loads[6].wait()

    @pl.when(mp > 0)
    def _():
        counts = recv_count[...]
        high = ((lane & 63) + 1).astype(F32)

        def used(b):
            return (iota((8, 128), 0) + b * 8) < counts

        slot_code[...] = invert(dst, used, lambda p: high, lambda p: ((lane >> 6) * 64 + p).astype(F32), 64).astype(I32)

    for i in range(2):
        wait_for(halo_in.at[i], halo_recv.at[i])
    for c in range(8):
        for i in range(2):
            work[c, 6 + i : 7 + i, :] = halo_in[0, i * 8 + c : i * 8 + c + 1, :]
            work[c, 72 + i : 73 + i, :] = halo_in[1, i * 8 + c : i * 8 + c + 1, :]
    for _ in range(2):
        sweep(work, 1, 1)
        sweep(work, 2, 0)

    @pl.when(magnetic)
    def _():
        wait_for(ar.at[pl.ds(0, 7)], recv.at[1])

    @pl.when(mp < 2)
    def _():
        wait_for(ar.at[pl.ds(0, 8)], recv.at[1])

    total = ar[0]
    for i in range(1, 8):
        total = total + ar[i]
    full[...] = total

    def give(i):
        push(full, spread.at[place], send.at[2], recv.at[2], in_plane(lax.rem(place + i, PLANE)))

    loop(PLANE // 2, PLANE, give)
    loop(1, PLANE // 2, give)
    spread[place] = total

    @pl.when(magnetic)
    def _():
        def used(b):
            return owner[pl.ds(b * 8, 8), :] == me

        def high(i):
            row = lax.rem(lax.div(i, 8), 4) * 32 + lax.rem(i, 2) * 16 + lax.div(i, 32) + 1
            return (row + (lane >> 5) * 4).astype(F32)

        def low(i):
            return (lax.rem(lax.div(i, 2), 4) * 32 + (lane & 31)).astype(F32)

        iono_code[...] = invert(cell, used, high, low, 128).astype(I32)

    loads[7].wait()
    wait_for(spread.at[pl.ds(0, PLANE - 1)], recv.at[2])
    acc = jnp.zeros((32, 128), F32)
    for i in range(128):
        acc = acc + response[:, i * 128 : (i + 1) * 128].astype(F32) * spread[i // 4, i % 4 : i % 4 + 1, :]
    tile[...] = jnp.zeros_like(tile)
    tile[pl.ds(pl.multiple_of(z * 32, 32), 32), :] = acc
    line[...] = jnp.sum(tile[...].T, axis=0, keepdims=True)

    def report(i):
        push(line, lines.at[level], send.at[3], recv.at[3], in_column(8 + lax.rem(level + i, 8)))

    @pl.when(magnetic)
    def _():
        loop(1, 8, report)
        lines[level] = line[...]

    @pl.when(mp < 2)
    def _():
        loop(0, 8, report)

    def forward(to_x, t, first):
        def one(i):
            to = lax.rem(yc + i, YC)
            push(mid.at[to_x, :, to], inbox.at[x, :, yc], fwd_send.at[t], inbox_recv.at[t], in_plane(to_x * YC + to))

        loop(first, YC, one)

    @pl.when(mp > 0)
    def _():
        wait_for(mid.at[pl.ds(0, 2)], mid_recv.at[0])
        forward(halves[0], 0, 0)
        forward(halves[0] + 2, 0, 0)

    @pl.when(magnetic)
    def _():
        wait_for(lines.at[pl.ds(0, LEVELS - 1)], recv.at[3])
        rows = []
        for m in range(4):
            row = lines[m * 4]
            for i in range(1, 4):
                row = row + lines[m * 4 + i]
            rows.append(row)
        mine = jnp.concatenate(rows, axis=0)
        pot_part[...] = mine

        def one(i):
            push(pot_part, pot.at[place], send.at[4], recv.at[4], in_plane(lax.rem(place + i, PLANE)))

        loop(PLANE // 2, PLANE, one)
        loop(1, PLANE // 2, one)
        pot[place] = mine

    def unpack(half):
        for i in range(4):
            for q in range(4):
                first = inbox[half, i, :, q, :]
                second = inbox[half + 2, i, :, q, :]
                table[2 * q, i * 8 : i * 8 + 8, :] = jnp.where(low, first, pltpu.roll(second, 64, 1))
                table[2 * q + 1, i * 8 : i * 8 + 8, :] = jnp.where(low, pltpu.roll(first, 64, 1), second)

        def block(b):
            at = pl.ds(pl.multiple_of(8 + b * 16, 8), 16)
            row = slot_code[pl.ds(b * 16, 16), :] - (1 + half * 32)
            spot = slot_code[pl.ds(64 + b * 16, 16), :]
            got = pick(
                lambda r: tuple(table[c, r : r + 1, :] for c in range(8)),
                32, row, spot, [work[c, at, :] for c in range(8)],
            )
            for c in range(8):
                work[c, at, :] = got[c]

        loop(0, 4, block)

    @pl.when(mp > 0)
    def _():
        wait_for(mid.at[pl.ds(0, 2)], mid_recv.at[1])
        forward(lax.rem(x + 2, 4), 1, 0)
        forward(x, 1, 1)
        inbox[x, :, yc] = mid[x, :, yc]
        wait_for(inbox.at[pl.ds(0, 2)], inbox_recv.at[0])
        unpack(halves[0])
        wait_for(inbox.at[pl.ds(0, 3), :, pl.ds(0, 5)], inbox_recv.at[1])
        unpack(halves[1])

    @pl.when(magnetic)
    def _():
        wait_for(pot.at[pl.ds(0, PLANE - 1)], recv.at[4])

        def block(b):
            at = pl.ds(pl.multiple_of(8 + b * 16, 8), 16)
            row = iono_code[pl.ds(b * 16, 16), :] - 1
            spot = iono_code[pl.ds(64 + b * 16, 16), :]
            (got,) = pick(
                lambda r: (pot[r // 4, r % 4 : r % 4 + 1, :],), 128, row, spot, [jnp.zeros((16, 128), F32)]
            )
            work[1, at, :] = work[1, at, :] + jnp.where(row >= 0, 0.5 * work[0, at, :] * got, 0.0)

        loop(0, 4, block)

    results = [
        pltpu.make_async_copy(work.at[0, body], density_out.at[0], load.at[0]),
        pltpu.make_async_copy(work.at[pl.ds(1, 7), body], fields_out.at[0], load.at[1]),
    ]
    for copy in results:
        copy.start()

    for i in range(2):
        wait_for(halo_out.at[i], halo_send.at[i])
    wait_for(spread.at[pl.ds(0, PLANE - 1)], send.at[2])

    @pl.when(mp < 3)
    def _():
        wait_for(mid, out_send)

    @pl.when(mp > 0)
    def _():
        wait_for(inbox.at[pl.ds(0, 2)], fwd_send.at[0])
        wait_for(inbox.at[pl.ds(0, 3), :, pl.ds(0, 5)], fwd_send.at[1])

    @pl.when(magnetic)
    def _():
        wait_for(rs.at[pl.ds(0, PLANE - 1)], send.at[0])
        wait_for(ar.at[pl.ds(0, LEVELS - 1)], send.at[1])
        wait_for(lines.at[pl.ds(0, 7)], send.at[3])
        wait_for(pot.at[pl.ds(0, PLANE - 1)], send.at[4])

    @pl.when(mp < 2)
    def _():
        wait_for(lines.at[pl.ds(0, 8)], send.at[3])

    for copy in results:
        copy.wait()


def local(density, fields, src_points, dst_points, recv_count, iono_owner, iono_cell, response):
    vmem = pltpu.VMEM
    dma = pltpu.SemaphoreType.DMA
    hbm = pl.BlockSpec(memory_space=pl.ANY)
    return pl.pallas_call(
        cycle_kernel,
        out_shape=[jax.ShapeDtypeStruct((1, 64, 128), F32), jax.ShapeDtypeStruct((1, 7, 64, 128), F32)],
        in_specs=[hbm] * 8,
        out_specs=[hbm] * 2,
        scratch_shapes=[
            vmem((8, 80, 128), F32),
            vmem((64, 128), I32),
            vmem((64, 128), I32),
            vmem((1, 128), I32),
            vmem((128, 128), I32),
            vmem((128, 128), I32),
            vmem((32, 16384), BF16),
            vmem((64, 128), I32),
            vmem((64, 128), F32),
            vmem((2, 16, 128), F32),
            vmem((2, 16, 128), F32),
            vmem((4, ZS, YC, 4, 128), F32),
            vmem((4, ZS, YC, 4, 128), F32),
            vmem((4, ZS, YC, 4, 128), F32),
            vmem((8, 32, 128), F32),
            vmem((PLANE, 4, 128), F32),
            vmem((PLANE, 4, 128), F32),
            vmem((4, 128), F32),
            vmem((LEVELS, 4, 128), F32),
            vmem((4, 128), F32),
            vmem((PLANE, 4, 128), F32),
            vmem((128, 128), F32),
            vmem((1, 128), F32),
            vmem((LEVELS, 1, 128), F32),
            vmem((4, 128), F32),
            vmem((PLANE, 4, 128), F32),
            vmem((128, 128), I32),
            vmem((128, 128), I32),
            dma((8,)),
            dma((2,)),
            dma((2,)),
            dma((5,)),
            dma((5,)),
            dma,
            dma((2,)),
            dma((2,)),
            dma((2,)),
        ],
        compiler_params=pltpu.CompilerParams(
            collective_id=0, has_side_effects=True, vmem_limit_bytes=56 * 1024 * 1024
        ),
        name="cycle",
    )(
        density, fields, src_points[0, 0].T, dst_points[0, 0].T, recv_count[0],
        iono_owner.reshape(128, 128), iono_cell.reshape(128, 128), response,
    )


def solution(mesh):
    placed = (
        P("mp", "space", None),
        P("mp", None, "space", None),
        P("mp", "space", None, None),
        P("mp", "space", None, None),
        P("mp", "space", None),
        P(),
        P(),
        P(("mp", "space"), None),
    )
    return jax.shard_map(
        local,
        mesh=mesh,
        in_specs=placed,
        out_specs=(P("mp", "space", None), P("mp", None, "space", None)),
        check_vma=False,
    )
```

```python
import jax
import jax.numpy as jnp
from jax import lax
from jax.experimental import pallas as pl
from jax.experimental.pallas import tpu as pltpu
from jax.sharding import PartitionSpec as P

MESH = pl.DeviceIdType.MESH
YC = 8
ZS = 4
SPACE = 128
PLANE = 32
LEVELS = 16
LAMBDA_STEP = 0.1
F32 = jnp.float32
I32 = jnp.int32
BF16 = jnp.bfloat16


def iota(shape, dim):
    return lax.broadcasted_iota(I32, shape, dim)


def loop(first, last, body):
    def step(i, carry):
        body(i)
        return carry

    lax.fori_loop(first, last, step, 0)


def wait_for(ref, sem):
    pltpu.make_async_copy(ref, ref, sem).wait()


def push(src_ref, dst_ref, send_sem, recv_sem, device):
    pltpu.make_async_remote_copy(
        src_ref=src_ref,
        dst_ref=dst_ref,
        send_sem=send_sem,
        recv_sem=recv_sem,
        device_id=device,
        device_id_type=MESH,
    ).start()


def pick(lines, count, row, lane, held):
    shape = row.shape
    for r in range(count):
        hit = row == r
        held = [
            jnp.where(
                hit,
                jnp.take_along_axis(jnp.broadcast_to(line, shape), lane, axis=1, mode="promise_in_bounds"),
                old,
            )
            for line, old in zip(lines(r), held)
        ]
    return held


def invert(rows_ref, used, high_of, low_of, count):
    def step(b, total):
        cells = rows_ref[pl.ds(b * 8, 8), :]
        row8 = jnp.where(used(b), cells >> 7, -1)
        col8 = cells & 127
        left, right = [], []
        for s in range(8):
            hit = iota((64, 128), 0) == row8[s : s + 1]
            left.append(
                jnp.concatenate(
                    [jnp.where(hit, high_of(b * 8 + s), 0.0), jnp.where(hit, low_of(b * 8 + s), 0.0)], axis=0
                ).astype(BF16)
            )
            right.append(jnp.where(iota((128, 128), 0) == col8[s : s + 1], 1.0, 0.0).astype(BF16))
        return total + lax.dot_general(
            jnp.concatenate(left, axis=1),
            jnp.concatenate(right, axis=1),
            (((1,), (1,)), ((), ())),
            preferred_element_type=F32,
        )

    return lax.fori_loop(0, count // 8, step, jnp.zeros((128, 128), F32))


def sweep(work, speed, axis):
    shape = (80, 128)
    size = shape[axis]
    at = iota(shape, axis)

    def above(value):
        moved = pltpu.roll(value, size - 1, axis)
        return jnp.where(at == size - 1, value, moved) if axis == 1 else moved

    u = work[speed] / work[0]
    u_up = above(u)
    fast = 0.5 * (jnp.maximum(jnp.abs(u), jnp.abs(u_up)) + 1.0)
    for c in range(8):
        q = work[c]
        flux = u * q
        face = 0.5 * (flux + above(flux)) - fast * (above(q) - q)
        below = pltpu.roll(face, 1, axis)
        if axis == 1:
            below = jnp.where(at == 0, flux, below)
        work[c] = q - LAMBDA_STEP * (face - below)


def cycle_kernel(
    density_in, fields_in, src_in, dst_in, count_in, owner_in, cell_in, response_in,
    density_out, fields_out,
    work, src, dst, recv_count, owner, cell, response, index, current, halo_out, halo_in,
    outbox, mid, inbox, table, contribution, rs, part, ar, full, spread, tile, line, lines, pot_part, pot,
    slot_code, iono_code,
    load, halo_send, halo_recv, send, recv, out_send, mid_recv, fwd_send, inbox_recv,
):
    mp = lax.axis_index("mp")
    space = lax.axis_index("space")
    x = lax.div(space, ZS * YC)
    z = lax.rem(lax.div(space, YC), ZS)
    yc = lax.rem(space, YC)
    place = x * YC + yc
    level = mp * ZS + z
    magnetic = mp >= 2
    me = (mp - 2) * SPACE + space

    def in_plane(p):
        return (mp, (lax.div(p, YC) * ZS + z) * YC + lax.rem(p, YC))

    def in_column(l):
        return (lax.div(l, ZS), (x * ZS + lax.rem(l, ZS)) * YC + yc)

    body = pl.ds(8, 64)
    loads = [
        pltpu.make_async_copy(a, b, load.at[i])
        for i, (a, b) in enumerate(
            (
                (fields_in.at[0], work.at[pl.ds(1, 7), body]),
                (density_in.at[0], work.at[0, body]),
                (cell_in, cell),
                (owner_in, owner),
                (src_in, src),
                (dst_in, dst),
                (count_in, recv_count),
                (response_in, response),
            )
        )
    ]
    for copy in loads:
        copy.start()

    barrier = pltpu.get_barrier_semaphore()

    def greet(device):
        pl.semaphore_signal(barrier, inc=1, device_id=device, device_id_type=MESH)

    after = (mp, lax.rem(space + 1, SPACE))
    before = (mp, lax.rem(space + SPACE - 1, SPACE))
    loop(1, LEVELS, lambda i: greet(in_column(lax.rem(level + i, LEVELS))))
    loop(1, PLANE, lambda i: greet(in_plane(lax.rem(place + i, PLANE))))
    greet(after)
    greet(before)

    low = iota((8, 128), 1) < 64
    lane = iota((1, 128), 1)
    for copy in loads[:4]:
        copy.wait()
    for c in range(8):
        work[c, 0:8, :] = jnp.ones((8, 128), F32)
        work[c, 72:80, :] = jnp.ones((8, 128), F32)

    @pl.when(magnetic)
    def _():
        b = work[6, 8:72, :]
        col = iota((64, 128), 1)
        right = jnp.where(col == 127, b, pltpu.roll(b, 127, 1))
        left = jnp.where(col == 0, b, pltpu.roll(b, 1, 1))
        current[...] = 0.5 * (right - left)

        def block(b):
            at = pl.ds(b * 16, 16)
            cells = cell[at, :]
            (got,) = pick(lambda r: (current[r : r + 1, :],), 64, cells >> 7, cells & 127, [jnp.zeros((16, 128), F32)])
            got = jnp.where(owner[at, :] == me, got, 0.0)
            for i in range(4):
                contribution[b * 4 + i] = got[i * 4 : i * 4 + 4]

        loop(0, 8, block)

    for c in range(8):
        for i in range(2):
            halo_out[0, i * 8 + c : i * 8 + c + 1, :] = work[c, 8 + i : 9 + i, :]
            halo_out[1, i * 8 + c : i * 8 + c + 1, :] = work[c, 70 + i : 71 + i, :]
    loads[4].wait()

    @pl.when(mp < 3)
    def _():
        points = src[...]
        turned = jnp.concatenate([points, points], axis=0).T
        index[...] = jnp.where(iota((64, 128), 1) < 64, turned[:64], turned[64:])

    def pack(half):
        def block(b):
            cells = index[pl.ds(half * 32 + b * 16, 16), :]
            got = pick(
                lambda r: tuple(work[c, 8 + r : 9 + r, :] for c in range(8)),
                64, cells >> 7, cells & 127, [jnp.zeros((16, 128), F32)] * 8,
            )
            for i in range(2):
                for q in range(4):
                    first = got[2 * q][i * 8 : i * 8 + 8]
                    second = got[2 * q + 1][i * 8 : i * 8 + 8]
                    outbox[half, b * 2 + i, :, q, :] = jnp.where(low, first, pltpu.roll(second, 64, 1))
                    outbox[half + 2, b * 2 + i, :, q, :] = jnp.where(low, pltpu.roll(first, 64, 1), second)

        loop(0, 2, block)

    def depart(to_x, t):
        def one(i):
            to = lax.rem(z + i, ZS)
            push(outbox.at[to_x, to], mid.at[to_x, z], out_send, mid_recv.at[t], in_column((mp + 1) * ZS + to))

        loop(0, ZS, one)

    halves = (lax.rem(x + 1, 2), lax.rem(x, 2))

    @pl.when(mp < 3)
    def _():
        pack(halves[0])

    pl.semaphore_wait(barrier, LEVELS - 1 + PLANE - 1 + 2)

    @pl.when(magnetic)
    def _():
        def one(i):
            to = lax.rem(place + i, PLANE)
            push(contribution.at[to], rs.at[place], send.at[0], recv.at[0], in_plane(to))

        loop(PLANE // 2, PLANE, one)
        loop(1, PLANE // 2, one)
        rs[place] = contribution[place]

    push(halo_out.at[0], halo_in.at[1], halo_send.at[0], halo_recv.at[1], before)
    push(halo_out.at[1], halo_in.at[0], halo_send.at[1], halo_recv.at[0], after)

    @pl.when(mp < 3)
    def _():
        depart(halves[0], 0)
        pack(halves[1])

    @pl.when(magnetic)
    def _():
        wait_for(rs.at[pl.ds(0, PLANE - 1)], recv.at[0])
        total = rs[0]
        for i in range(1, PLANE):
            total = total + rs[i]
        part[...] = total

        def one(i):
            push(part, ar.at[level - 8], send.at[1], recv.at[1], in_column(lax.rem(level + i, LEVELS)))

        loop(8, LEVELS, one)
        loop(1, 8, one)
        ar[level - 8] = total

    loads[5].wait()
    loads[6].wait()

    @pl.when(mp > 0)
    def _():
        counts = recv_count[...]
        high = ((lane & 63) + 1).astype(F32)

        def used(b):
            return (iota((8, 128), 0) + b * 8) < counts

        slot_code[...] = invert(dst, used, lambda p: high, lambda p: ((lane >> 6) * 64 + p).astype(F32), 64).astype(I32)

    @pl.when(mp < 3)
    def _():
        depart(halves[0] + 2, 0)

    for i in range(2):
        wait_for(halo_in.at[i], halo_recv.at[i])
    for c in range(8):
        for i in range(2):
            work[c, 6 + i : 7 + i, :] = halo_in[0, i * 8 + c : i * 8 + c + 1, :]
            work[c, 72 + i : 73 + i, :] = halo_in[1, i * 8 + c : i * 8 + c + 1, :]
    for _ in range(2):
        sweep(work, 1, 1)
        sweep(work, 2, 0)

    @pl.when(magnetic)
    def _():
        wait_for(ar.at[pl.ds(0, 7)], recv.at[1])

    @pl.when(mp < 2)
    def _():
        wait_for(ar.at[pl.ds(0, 8)], recv.at[1])

    total = ar[0]
    for i in range(1, 8):
        total = total + ar[i]
    full[...] = total

    def give(i):
        push(full, spread.at[place], send.at[2], recv.at[2], in_plane(lax.rem(place + i, PLANE)))

    loop(PLANE // 2, PLANE, give)
    loop(1, PLANE // 2, give)
    spread[place] = total

    @pl.when(mp < 3)
    def _():
        depart(lax.rem(x + 2, 4), 1)

    @pl.when(magnetic)
    def _():
        def used(b):
            return owner[pl.ds(b * 8, 8), :] == me

        def high(i):
            row = lax.rem(lax.div(i, 8), 4) * 32 + lax.rem(i, 2) * 16 + lax.div(i, 32) + 1
            return (row + (lane >> 5) * 4).astype(F32)

        def low(i):
            return (lax.rem(lax.div(i, 2), 4) * 32 + (lane & 31)).astype(F32)

        iono_code[...] = invert(cell, used, high, low, 128).astype(I32)

    loads[7].wait()
    wait_for(spread.at[pl.ds(0, PLANE - 1)], recv.at[2])
    acc = jnp.zeros((32, 128), F32)
    for i in range(128):
        acc = acc + response[:, i * 128 : (i + 1) * 128].astype(F32) * spread[i // 4, i % 4 : i % 4 + 1, :]
    tile[...] = jnp.zeros_like(tile)
    tile[pl.ds(pl.multiple_of(z * 32, 32), 32), :] = acc
    line[...] = jnp.sum(tile[...].T, axis=0, keepdims=True)

    def report(i):
        push(line, lines.at[level], send.at[3], recv.at[3], in_column(8 + lax.rem(level + i, 8)))

    @pl.when(magnetic)
    def _():
        loop(1, 8, report)
        lines[level] = line[...]

    @pl.when(mp < 2)
    def _():
        loop(0, 8, report)

    def forward(to_x, t, first):
        def one(i):
            to = lax.rem(yc + i, YC)
            push(mid.at[to_x, :, to], inbox.at[x, :, yc], fwd_send.at[t], inbox_recv.at[t], in_plane(to_x * YC + to))

        loop(first, YC, one)

    @pl.when(mp < 3)
    def _():
        depart(x, 1)

    @pl.when(mp > 0)
    def _():
        wait_for(mid.at[pl.ds(0, 2)], mid_recv.at[0])
        forward(halves[0], 0, 0)
        forward(halves[0] + 2, 0, 0)

    @pl.when(magnetic)
    def _():
        wait_for(lines.at[pl.ds(0, LEVELS - 1)], recv.at[3])
        rows = []
        for m in range(4):
            row = lines[m * 4]
            for i in range(1, 4):
                row = row + lines[m * 4 + i]
            rows.append(row)
        mine = jnp.concatenate(rows, axis=0)
        pot_part[...] = mine

        def one(i):
            push(pot_part, pot.at[place], send.at[4], recv.at[4], in_plane(lax.rem(place + i, PLANE)))

        loop(PLANE // 2, PLANE, one)
        loop(1, PLANE // 2, one)
        pot[place] = mine

    def unpack(half):
        for i in range(4):
            for q in range(4):
                first = inbox[half, i, :, q, :]
                second = inbox[half + 2, i, :, q, :]
                table[2 * q, i * 8 : i * 8 + 8, :] = jnp.where(low, first, pltpu.roll(second, 64, 1))
                table[2 * q + 1, i * 8 : i * 8 + 8, :] = jnp.where(low, pltpu.roll(first, 64, 1), second)

        def block(b):
            at = pl.ds(pl.multiple_of(8 + b * 16, 8), 16)
            row = slot_code[pl.ds(b * 16, 16), :] - (1 + half * 32)
            spot = slot_code[pl.ds(64 + b * 16, 16), :]
            got = pick(
                lambda r: tuple(table[c, r : r + 1, :] for c in range(8)),
                32, row, spot, [work[c, at, :] for c in range(8)],
            )
            for c in range(8):
                work[c, at, :] = got[c]

        loop(0, 4, block)

    @pl.when(mp > 0)
    def _():
        wait_for(mid.at[pl.ds(0, 2)], mid_recv.at[1])
        forward(lax.rem(x + 2, 4), 1, 0)
        forward(x, 1, 1)
        inbox[x, :, yc] = mid[x, :, yc]
        wait_for(inbox.at[pl.ds(0, 2)], inbox_recv.at[0])
        unpack(halves[0])
        wait_for(inbox.at[pl.ds(0, 3), :, pl.ds(0, 5)], inbox_recv.at[1])
        unpack(halves[1])

    @pl.when(magnetic)
    def _():
        wait_for(pot.at[pl.ds(0, PLANE - 1)], recv.at[4])

        def block(b):
            at = pl.ds(pl.multiple_of(8 + b * 16, 8), 16)
            row = iono_code[pl.ds(b * 16, 16), :] - 1
            spot = iono_code[pl.ds(64 + b * 16, 16), :]
            (got,) = pick(
                lambda r: (pot[r // 4, r % 4 : r % 4 + 1, :],), 128, row, spot, [jnp.zeros((16, 128), F32)]
            )
            work[1, at, :] = work[1, at, :] + jnp.where(row >= 0, 0.5 * work[0, at, :] * got, 0.0)

        loop(0, 4, block)

    results = [
        pltpu.make_async_copy(work.at[0, body], density_out.at[0], load.at[0]),
        pltpu.make_async_copy(work.at[pl.ds(1, 7), body], fields_out.at[0], load.at[1]),
    ]
    for copy in results:
        copy.start()

    for i in range(2):
        wait_for(halo_out.at[i], halo_send.at[i])
    wait_for(spread.at[pl.ds(0, PLANE - 1)], send.at[2])

    @pl.when(mp < 3)
    def _():
        wait_for(mid, out_send)

    @pl.when(mp > 0)
    def _():
        wait_for(inbox.at[pl.ds(0, 2)], fwd_send.at[0])
        wait_for(inbox.at[pl.ds(0, 3), :, pl.ds(0, 5)], fwd_send.at[1])

    @pl.when(magnetic)
    def _():
        wait_for(rs.at[pl.ds(0, PLANE - 1)], send.at[0])
        wait_for(ar.at[pl.ds(0, LEVELS - 1)], send.at[1])
        wait_for(lines.at[pl.ds(0, 7)], send.at[3])
        wait_for(pot.at[pl.ds(0, PLANE - 1)], send.at[4])

    @pl.when(mp < 2)
    def _():
        wait_for(lines.at[pl.ds(0, 8)], send.at[3])

    for copy in results:
        copy.wait()


def local(density, fields, src_points, dst_points, recv_count, iono_owner, iono_cell, response):
    vmem = pltpu.VMEM
    dma = pltpu.SemaphoreType.DMA
    hbm = pl.BlockSpec(memory_space=pl.ANY)
    return pl.pallas_call(
        cycle_kernel,
        out_shape=[jax.ShapeDtypeStruct((1, 64, 128), F32), jax.ShapeDtypeStruct((1, 7, 64, 128), F32)],
        in_specs=[hbm] * 8,
        out_specs=[hbm] * 2,
        scratch_shapes=[
            vmem((8, 80, 128), F32),
            vmem((64, 128), I32),
            vmem((64, 128), I32),
            vmem((1, 128), I32),
            vmem((128, 128), I32),
            vmem((128, 128), I32),
            vmem((32, 16384), BF16),
            vmem((64, 128), I32),
            vmem((64, 128), F32),
            vmem((2, 16, 128), F32),
            vmem((2, 16, 128), F32),
            vmem((4, ZS, YC, 4, 128), F32),
            vmem((4, ZS, YC, 4, 128), F32),
            vmem((4, ZS, YC, 4, 128), F32),
            vmem((8, 32, 128), F32),
            vmem((PLANE, 4, 128), F32),
            vmem((PLANE, 4, 128), F32),
            vmem((4, 128), F32),
            vmem((LEVELS, 4, 128), F32),
            vmem((4, 128), F32),
            vmem((PLANE, 4, 128), F32),
            vmem((128, 128), F32),
            vmem((1, 128), F32),
            vmem((LEVELS, 1, 128), F32),
            vmem((4, 128), F32),
            vmem((PLANE, 4, 128), F32),
            vmem((128, 128), I32),
            vmem((128, 128), I32),
            dma((8,)),
            dma((2,)),
            dma((2,)),
            dma((5,)),
            dma((5,)),
            dma,
            dma((2,)),
            dma((2,)),
            dma((2,)),
        ],
        compiler_params=pltpu.CompilerParams(
            collective_id=0, has_side_effects=True, vmem_limit_bytes=56 * 1024 * 1024
        ),
        name="cycle",
    )(
        density, fields, src_points[0, 0].T, dst_points[0, 0].T, recv_count[0],
        iono_owner.reshape(128, 128), iono_cell.reshape(128, 128), response,
    )


def solution(mesh):
    placed = (
        P("mp", "space", None),
        P("mp", None, "space", None),
        P("mp", "space", None, None),
        P("mp", "space", None, None),
        P("mp", "space", None),
        P(),
        P(),
        P(("mp", "space"), None),
    )
    return jax.shard_map(
        local,
        mesh=mesh,
        in_specs=placed,
        out_specs=(P("mp", "space", None), P("mp", None, "space", None)),
        check_vma=False,
    )
```

```python
import jax
import jax.numpy as jnp
from jax import lax
from jax.experimental import pallas as pl
from jax.experimental.pallas import tpu as pltpu
from jax.sharding import PartitionSpec as P

MESH = pl.DeviceIdType.MESH
YC = 8
ZS = 4
SPACE = 128
PLANE = 32
LEVELS = 16
LAMBDA_STEP = 0.1
F32 = jnp.float32
I32 = jnp.int32
BF16 = jnp.bfloat16


def iota(shape, dim):
    return lax.broadcasted_iota(I32, shape, dim)


def loop(first, last, body):
    def step(i, carry):
        body(i)
        return carry

    lax.fori_loop(first, last, step, 0)


def wait_for(ref, sem):
    pltpu.make_async_copy(ref, ref, sem).wait()


def push(src_ref, dst_ref, send_sem, recv_sem, device):
    pltpu.make_async_remote_copy(
        src_ref=src_ref,
        dst_ref=dst_ref,
        send_sem=send_sem,
        recv_sem=recv_sem,
        device_id=device,
        device_id_type=MESH,
    ).start()


def pick(lines, count, row, lane, held):
    shape = row.shape
    for r in range(count):
        hit = row == r
        held = [
            jnp.where(
                hit,
                jnp.take_along_axis(jnp.broadcast_to(line, shape), lane, axis=1, mode="promise_in_bounds"),
                old,
            )
            for line, old in zip(lines(r), held)
        ]
    return held


def invert(rows_ref, used, high_of, low_of, count):
    def step(b, total):
        cells = rows_ref[pl.ds(b * 8, 8), :]
        row8 = jnp.where(used(b), cells >> 7, -1)
        col8 = cells & 127
        left, right = [], []
        for s in range(8):
            hit = iota((64, 128), 0) == row8[s : s + 1]
            left.append(
                jnp.concatenate(
                    [jnp.where(hit, high_of(b * 8 + s), 0.0), jnp.where(hit, low_of(b * 8 + s), 0.0)], axis=0
                ).astype(BF16)
            )
            right.append(jnp.where(iota((128, 128), 0) == col8[s : s + 1], 1.0, 0.0).astype(BF16))
        return total + lax.dot_general(
            jnp.concatenate(left, axis=1),
            jnp.concatenate(right, axis=1),
            (((1,), (1,)), ((), ())),
            preferred_element_type=F32,
        )

    return lax.fori_loop(0, count // 8, step, jnp.zeros((128, 128), F32))


def sweep(work, speed, axis):
    shape = (80, 128)
    size = shape[axis]
    at = iota(shape, axis)

    def above(value):
        moved = pltpu.roll(value, size - 1, axis)
        return jnp.where(at == size - 1, value, moved) if axis == 1 else moved

    u = work[speed] / work[0]
    u_up = above(u)
    fast = 0.5 * (jnp.maximum(jnp.abs(u), jnp.abs(u_up)) + 1.0)
    for c in range(8):
        q = work[c]
        flux = u * q
        face = 0.5 * (flux + above(flux)) - fast * (above(q) - q)
        below = pltpu.roll(face, 1, axis)
        if axis == 1:
            below = jnp.where(at == 0, flux, below)
        work[c] = q - LAMBDA_STEP * (face - below)


def cycle_kernel(
    density_in, fields_in, src_in, dst_in, count_in, owner_in, cell_in, response_in,
    state_out,
    work, src, dst, recv_count, owner, cell, response, index, current, halo_out, halo_in,
    outbox, mid, inbox, table, contribution, rs, part, ar, full, spread, tile, line, lines, pot_part, pot,
    slot_code, iono_code,
    load, halo_send, halo_recv, send, recv, out_send, mid_recv, fwd_send, inbox_recv,
):
    mp = lax.axis_index("mp")
    space = lax.axis_index("space")
    x = lax.div(space, ZS * YC)
    z = lax.rem(lax.div(space, YC), ZS)
    yc = lax.rem(space, YC)
    place = x * YC + yc
    level = mp * ZS + z
    magnetic = mp >= 2
    me = (mp - 2) * SPACE + space

    def in_plane(p):
        return (mp, (lax.div(p, YC) * ZS + z) * YC + lax.rem(p, YC))

    def in_column(l):
        return (lax.div(l, ZS), (x * ZS + lax.rem(l, ZS)) * YC + yc)

    body = pl.ds(8, 64)
    loads = [
        pltpu.make_async_copy(a, b, load.at[i])
        for i, (a, b) in enumerate(
            (
                (fields_in.at[0], work.at[pl.ds(1, 7), body]),
                (density_in.at[0], work.at[0, body]),
                (cell_in, cell),
                (owner_in, owner),
                (src_in, src),
                (dst_in, dst),
                (count_in, recv_count),
                (response_in, response),
            )
        )
    ]
    for copy in loads:
        copy.start()

    barrier = pltpu.get_barrier_semaphore()

    def greet(device):
        pl.semaphore_signal(barrier, inc=1, device_id=device, device_id_type=MESH)

    after = (mp, lax.rem(space + 1, SPACE))
    before = (mp, lax.rem(space + SPACE - 1, SPACE))
    loop(1, LEVELS, lambda i: greet(in_column(lax.rem(level + i, LEVELS))))
    loop(1, PLANE, lambda i: greet(in_plane(lax.rem(place + i, PLANE))))
    greet(after)
    greet(before)

    low = iota((8, 128), 1) < 64
    lane = iota((1, 128), 1)
    for copy in loads[:4]:
        copy.wait()
    for c in range(8):
        work[c, 0:8, :] = jnp.ones((8, 128), F32)
        work[c, 72:80, :] = jnp.ones((8, 128), F32)

    @pl.when(magnetic)
    def _():
        b = work[6, 8:72, :]
        col = iota((64, 128), 1)
        right = jnp.where(col == 127, b, pltpu.roll(b, 127, 1))
        left = jnp.where(col == 0, b, pltpu.roll(b, 1, 1))
        current[...] = 0.5 * (right - left)

        def block(b):
            at = pl.ds(b * 16, 16)
            cells = cell[at, :]
            (got,) = pick(lambda r: (current[r : r + 1, :],), 64, cells >> 7, cells & 127, [jnp.zeros((16, 128), F32)])
            got = jnp.where(owner[at, :] == me, got, 0.0)
            for i in range(4):
                contribution[b * 4 + i] = got[i * 4 : i * 4 + 4]

        loop(0, 8, block)

    for c in range(8):
        for i in range(2):
            halo_out[0, i * 8 + c : i * 8 + c + 1, :] = work[c, 8 + i : 9 + i, :]
            halo_out[1, i * 8 + c : i * 8 + c + 1, :] = work[c, 70 + i : 71 + i, :]
    loads[4].wait()

    @pl.when(mp < 3)
    def _():
        points = src[...]
        turned = jnp.concatenate([points, points], axis=0).T
        index[...] = jnp.where(iota((64, 128), 1) < 64, turned[:64], turned[64:])

    def pack(half):
        def block(b):
            cells = index[pl.ds(half * 32 + b * 16, 16), :]
            got = pick(
                lambda r: tuple(work[c, 8 + r : 9 + r, :] for c in range(8)),
                64, cells >> 7, cells & 127, [jnp.zeros((16, 128), F32)] * 8,
            )
            for i in range(2):
                for q in range(4):
                    first = got[2 * q][i * 8 : i * 8 + 8]
                    second = got[2 * q + 1][i * 8 : i * 8 + 8]
                    outbox[half, b * 2 + i, :, q, :] = jnp.where(low, first, pltpu.roll(second, 64, 1))
                    outbox[half + 2, b * 2 + i, :, q, :] = jnp.where(low, pltpu.roll(first, 64, 1), second)

        loop(0, 2, block)

    def depart(to_x, t):
        def one(i):
            to = lax.rem(z + i, ZS)
            push(outbox.at[to_x, to], mid.at[to_x, z], out_send, mid_recv.at[t], in_column((mp + 1) * ZS + to))

        loop(0, ZS, one)

    halves = (lax.rem(x + 1, 2), lax.rem(x, 2))

    @pl.when(mp < 3)
    def _():
        pack(halves[0])

    pl.semaphore_wait(barrier, LEVELS - 1 + PLANE - 1 + 2)

    @pl.when(magnetic)
    def _():
        def one(i):
            to = lax.rem(place + i, PLANE)
            push(contribution.at[to], rs.at[place], send.at[0], recv.at[0], in_plane(to))

        loop(PLANE // 2, PLANE, one)
        loop(1, PLANE // 2, one)
        rs[place] = contribution[place]

    push(halo_out.at[0], halo_in.at[1], halo_send.at[0], halo_recv.at[1], before)
    push(halo_out.at[1], halo_in.at[0], halo_send.at[1], halo_recv.at[0], after)

    @pl.when(mp < 3)
    def _():
        depart(halves[0], 0)
        pack(halves[1])

    @pl.when(magnetic)
    def _():
        wait_for(rs.at[pl.ds(0, PLANE - 1)], recv.at[0])
        total = rs[0]
        for i in range(1, PLANE):
            total = total + rs[i]
        part[...] = total

        def one(i):
            push(part, ar.at[level - 8], send.at[1], recv.at[1], in_column(lax.rem(level + i, LEVELS)))

        loop(8, LEVELS, one)
        loop(1, 8, one)
        ar[level - 8] = total

    loads[5].wait()
    loads[6].wait()

    @pl.when(mp > 0)
    def _():
        counts = recv_count[...]
        high = ((lane & 63) + 1).astype(F32)

        def used(b):
            return (iota((8, 128), 0) + b * 8) < counts

        slot_code[...] = invert(dst, used, lambda p: high, lambda p: ((lane >> 6) * 64 + p).astype(F32), 64).astype(I32)

    @pl.when(mp < 3)
    def _():
        depart(halves[0] + 2, 0)

    for i in range(2):
        wait_for(halo_in.at[i], halo_recv.at[i])
    for c in range(8):
        for i in range(2):
            work[c, 6 + i : 7 + i, :] = halo_in[0, i * 8 + c : i * 8 + c + 1, :]
            work[c, 72 + i : 73 + i, :] = halo_in[1, i * 8 + c : i * 8 + c + 1, :]
    for _ in range(2):
        sweep(work, 1, 1)
        sweep(work, 2, 0)

    @pl.when(magnetic)
    def _():
        wait_for(ar.at[pl.ds(0, 7)], recv.at[1])

    @pl.when(mp < 2)
    def _():
        wait_for(ar.at[pl.ds(0, 8)], recv.at[1])

    total = ar[0]
    for i in range(1, 8):
        total = total + ar[i]
    full[...] = total

    def give(i):
        push(full, spread.at[place], send.at[2], recv.at[2], in_plane(lax.rem(place + i, PLANE)))

    loop(PLANE // 2, PLANE, give)
    loop(1, PLANE // 2, give)
    spread[place] = total

    @pl.when(mp < 3)
    def _():
        depart(lax.rem(x + 2, 4), 1)

    @pl.when(magnetic)
    def _():
        def used(b):
            return owner[pl.ds(b * 8, 8), :] == me

        def high(i):
            row = lax.rem(lax.div(i, 8), 4) * 32 + lax.rem(i, 2) * 16 + lax.div(i, 32) + 1
            return (row + (lane >> 5) * 4).astype(F32)

        def low(i):
            return (lax.rem(lax.div(i, 2), 4) * 32 + (lane & 31)).astype(F32)

        iono_code[...] = invert(cell, used, high, low, 128).astype(I32)

    loads[7].wait()
    wait_for(spread.at[pl.ds(0, PLANE - 1)], recv.at[2])
    acc = jnp.zeros((32, 128), F32)
    for i in range(128):
        acc = acc + response[:, i * 128 : (i + 1) * 128].astype(F32) * spread[i // 4, i % 4 : i % 4 + 1, :]
    tile[...] = jnp.zeros_like(tile)
    tile[pl.ds(pl.multiple_of(z * 32, 32), 32), :] = acc
    line[...] = jnp.sum(tile[...].T, axis=0, keepdims=True)

    def report(i):
        push(line, lines.at[level], send.at[3], recv.at[3], in_column(8 + lax.rem(level + i, 8)))

    @pl.when(magnetic)
    def _():
        loop(1, 8, report)
        lines[level] = line[...]

    @pl.when(mp < 2)
    def _():
        loop(0, 8, report)

    def forward(to_x, t, first):
        def one(i):
            to = lax.rem(yc + i, YC)
            push(mid.at[to_x, :, to], inbox.at[x, :, yc], fwd_send.at[t], inbox_recv.at[t], in_plane(to_x * YC + to))

        loop(first, YC, one)

    @pl.when(mp < 3)
    def _():
        depart(x, 1)

    @pl.when(mp > 0)
    def _():
        wait_for(mid.at[pl.ds(0, 2)], mid_recv.at[0])
        forward(halves[0], 0, 0)
        forward(halves[0] + 2, 0, 0)

    @pl.when(magnetic)
    def _():
        wait_for(lines.at[pl.ds(0, LEVELS - 1)], recv.at[3])
        rows = []
        for m in range(4):
            row = lines[m * 4]
            for i in range(1, 4):
                row = row + lines[m * 4 + i]
            rows.append(row)
        mine = jnp.concatenate(rows, axis=0)
        pot_part[...] = mine

        def one(i):
            push(pot_part, pot.at[place], send.at[4], recv.at[4], in_plane(lax.rem(place + i, PLANE)))

        loop(PLANE // 2, PLANE, one)
        loop(1, PLANE // 2, one)
        pot[place] = mine

    def unpack(half):
        for i in range(4):
            for q in range(4):
                first = inbox[half, i, :, q, :]
                second = inbox[half + 2, i, :, q, :]
                table[2 * q, i * 8 : i * 8 + 8, :] = jnp.where(low, first, pltpu.roll(second, 64, 1))
                table[2 * q + 1, i * 8 : i * 8 + 8, :] = jnp.where(low, pltpu.roll(first, 64, 1), second)

        def block(b):
            at = pl.ds(pl.multiple_of(8 + b * 16, 8), 16)
            row = slot_code[pl.ds(b * 16, 16), :] - (1 + half * 32)
            spot = slot_code[pl.ds(64 + b * 16, 16), :]
            got = pick(
                lambda r: tuple(table[c, r : r + 1, :] for c in range(8)),
                32, row, spot, [work[c, at, :] for c in range(8)],
            )
            for c in range(8):
                work[c, at, :] = got[c]

        loop(0, 4, block)

    @pl.when(mp > 0)
    def _():
        wait_for(mid.at[pl.ds(0, 2)], mid_recv.at[1])
        forward(lax.rem(x + 2, 4), 1, 0)
        forward(x, 1, 1)
        inbox[x, :, yc] = mid[x, :, yc]
        wait_for(inbox.at[pl.ds(0, 2)], inbox_recv.at[0])
        unpack(halves[0])

    @pl.when(magnetic)
    def _():
        wait_for(pot.at[pl.ds(0, PLANE - 1)], recv.at[4])

        def block(b):
            row = iono_code[pl.ds(b * 16, 16), :] - 1
            spot = iono_code[pl.ds(64 + b * 16, 16), :]
            (got,) = pick(
                lambda r: (pot[r // 4, r % 4 : r % 4 + 1, :],), 128, row, spot, [jnp.zeros((16, 128), F32)]
            )
            current[pl.ds(b * 16, 16), :] = 0.5 * got

        loop(0, 4, block)

    @pl.when(mp > 0)
    def _():
        wait_for(inbox.at[pl.ds(0, 3), :, pl.ds(0, 5)], inbox_recv.at[1])
        unpack(halves[1])

    @pl.when(magnetic)
    def _():
        work[1, body, :] = work[1, body, :] + work[0, body, :] * current[...]


    state_out[...] = work[:, 8:72, :]

    for i in range(2):
        wait_for(halo_out.at[i], halo_send.at[i])
    wait_for(spread.at[pl.ds(0, PLANE - 1)], send.at[2])

    @pl.when(mp < 3)
    def _():
        wait_for(mid, out_send)

    @pl.when(mp > 0)
    def _():
        wait_for(inbox.at[pl.ds(0, 2)], fwd_send.at[0])
        wait_for(inbox.at[pl.ds(0, 3), :, pl.ds(0, 5)], fwd_send.at[1])

    @pl.when(magnetic)
    def _():
        wait_for(rs.at[pl.ds(0, PLANE - 1)], send.at[0])
        wait_for(ar.at[pl.ds(0, LEVELS - 1)], send.at[1])
        wait_for(lines.at[pl.ds(0, 7)], send.at[3])
        wait_for(pot.at[pl.ds(0, PLANE - 1)], send.at[4])

    @pl.when(mp < 2)
    def _():
        wait_for(lines.at[pl.ds(0, 8)], send.at[3])


def hand_out(state, density_out, fields_out, sem):
    copies = [
        pltpu.make_async_copy(state.at[0], density_out.at[0], sem.at[0]),
        pltpu.make_async_copy(state.at[pl.ds(1, 7)], fields_out.at[0], sem.at[1]),
    ]
    for copy in copies:
        copy.start()
    for copy in copies:
        copy.wait()


def local(density, fields, src_points, dst_points, recv_count, iono_owner, iono_cell, response):
    vmem = pltpu.VMEM
    dma = pltpu.SemaphoreType.DMA
    hbm = pl.BlockSpec(memory_space=pl.ANY)
    state = pl.pallas_call(
        cycle_kernel,
        out_shape=vmem((8, 64, 128), F32),
        in_specs=[hbm] * 8,
        out_specs=pl.BlockSpec(memory_space=vmem),
        scratch_shapes=[
            vmem((8, 80, 128), F32),
            vmem((64, 128), I32),
            vmem((64, 128), I32),
            vmem((1, 128), I32),
            vmem((128, 128), I32),
            vmem((128, 128), I32),
            vmem((32, 16384), BF16),
            vmem((64, 128), I32),
            vmem((64, 128), F32),
            vmem((2, 16, 128), F32),
            vmem((2, 16, 128), F32),
            vmem((4, ZS, YC, 4, 128), F32),
            vmem((4, ZS, YC, 4, 128), F32),
            vmem((4, ZS, YC, 4, 128), F32),
            vmem((8, 32, 128), F32),
            vmem((PLANE, 4, 128), F32),
            vmem((PLANE, 4, 128), F32),
            vmem((4, 128), F32),
            vmem((LEVELS, 4, 128), F32),
            vmem((4, 128), F32),
            vmem((PLANE, 4, 128), F32),
            vmem((128, 128), F32),
            vmem((1, 128), F32),
            vmem((LEVELS, 1, 128), F32),
            vmem((4, 128), F32),
            vmem((PLANE, 4, 128), F32),
            vmem((128, 128), I32),
            vmem((128, 128), I32),
            dma((8,)),
            dma((2,)),
            dma((2,)),
            dma((5,)),
            dma((5,)),
            dma,
            dma((2,)),
            dma((2,)),
            dma((2,)),
        ],
        compiler_params=pltpu.CompilerParams(
            collective_id=0, has_side_effects=True, vmem_limit_bytes=56 * 1024 * 1024
        ),
        name="cycle",
    )(
        density, fields, src_points[0, 0].T, dst_points[0, 0].T, recv_count[0],
        iono_owner.reshape(128, 128), iono_cell.reshape(128, 128), response,
    )
    return state[:1], state[1:][None]


def solution(mesh):
    placed = (
        P("mp", "space", None),
        P("mp", None, "space", None),
        P("mp", "space", None, None),
        P("mp", "space", None, None),
        P("mp", "space", None),
        P(),
        P(),
        P(("mp", "space"), None),
    )
    return jax.shard_map(
        local,
        mesh=mesh,
        in_specs=placed,
        out_specs=(P("mp", "space", None), P("mp", None, "space", None)),
        check_vma=False,
    )
```

```python
import jax
import jax.numpy as jnp
from jax import lax
from jax.experimental import pallas as pl
from jax.experimental.pallas import tpu as pltpu
from jax.sharding import PartitionSpec as P

MESH = pl.DeviceIdType.MESH
YC = 8
ZS = 4
SPACE = 128
PLANE = 32
LEVELS = 16
ROUND = 2
LAMBDA_STEP = 0.1
F32 = jnp.float32
I32 = jnp.int32
BF16 = jnp.bfloat16


def iota(shape, dim):
    return lax.broadcasted_iota(I32, shape, dim)


def loop(first, last, body):
    def step(i, carry):
        body(i)
        return carry

    lax.fori_loop(first, last, step, 0)


def wait_for(ref, sem):
    pltpu.make_async_copy(ref, ref, sem).wait()


def push(src_ref, dst_ref, send_sem, recv_sem, device):
    pltpu.make_async_remote_copy(
        src_ref=src_ref,
        dst_ref=dst_ref,
        send_sem=send_sem,
        recv_sem=recv_sem,
        device_id=device,
        device_id_type=MESH,
    ).start()


def pick(lines, count, row, lane, held):
    shape = row.shape
    for r in range(count):
        hit = row == r
        held = [
            jnp.where(
                hit,
                jnp.take_along_axis(jnp.broadcast_to(line, shape), lane, axis=1, mode="promise_in_bounds"),
                old,
            )
            for line, old in zip(lines(r), held)
        ]
    return held


def invert(rows_ref, used, high_of, low_of, count):
    def step(b, total):
        cells = rows_ref[pl.ds(b * 8, 8), :]
        row8 = jnp.where(used(b), cells >> 7, -1)
        col8 = cells & 127
        left, right = [], []
        for s in range(8):
            hit = iota((64, 128), 0) == row8[s : s + 1]
            left.append(
                jnp.concatenate(
                    [jnp.where(hit, high_of(b * 8 + s), 0.0), jnp.where(hit, low_of(b * 8 + s), 0.0)], axis=0
                ).astype(BF16)
            )
            right.append(jnp.where(iota((128, 128), 0) == col8[s : s + 1], 1.0, 0.0).astype(BF16))
        return total + lax.dot_general(
            jnp.concatenate(left, axis=1),
            jnp.concatenate(right, axis=1),
            (((1,), (1,)), ((), ())),
            preferred_element_type=F32,
        )

    return lax.fori_loop(0, count // 8, step, jnp.zeros((128, 128), F32))


def sweep(work, speed, axis):
    shape = (80, 128)
    size = shape[axis]
    at = iota(shape, axis)

    def above(value):
        moved = pltpu.roll(value, size - 1, axis)
        return jnp.where(at == size - 1, value, moved) if axis == 1 else moved

    u = work[speed] / work[0]
    u_up = above(u)
    fast = 0.5 * (jnp.maximum(jnp.abs(u), jnp.abs(u_up)) + 1.0)
    for c in range(8):
        q = work[c]
        flux = u * q
        face = 0.5 * (flux + above(flux)) - fast * (above(q) - q)
        below = pltpu.roll(face, 1, axis)
        if axis == 1:
            below = jnp.where(at == 0, flux, below)
        work[c] = q - LAMBDA_STEP * (face - below)


def cycle_kernel(
    density_in, fields_in, src_in, dst_in, count_in, owner_in, cell_in, response_in,
    state_out,
    work, src, dst, recv_count, owner, cell, response, index, current, halo_out, halo_in,
    outbox, mid, inbox, relay, table, contribution, rs, part, ar, full, spread, tile, line, lines, pot_part, pot,
    slot_code, iono_code,
    load, halo_send, halo_recv, send, recv, out_send, mid_recv, fwd_send, inbox_recv, relay_send, relay_recv, known,
):
    mp = lax.axis_index("mp")
    space = lax.axis_index("space")
    x = lax.div(space, ZS * YC)
    z = lax.rem(lax.div(space, YC), ZS)
    yc = lax.rem(space, YC)
    place = x * YC + yc
    level = mp * ZS + z
    magnetic = mp >= 2
    me = (mp - 2) * SPACE + space

    def in_plane(p):
        return (mp, (lax.div(p, YC) * ZS + z) * YC + lax.rem(p, YC))

    def in_column(l):
        return (lax.div(l, ZS), (x * ZS + lax.rem(l, ZS)) * YC + yc)

    body = pl.ds(8, 64)
    loads = [
        pltpu.make_async_copy(a, b, load.at[i])
        for i, (a, b) in enumerate(
            (
                (fields_in.at[0], work.at[pl.ds(1, 7), body]),
                (density_in.at[0], work.at[0, body]),
                (cell_in, cell),
                (owner_in, owner),
                (src_in, src),
                (dst_in, dst),
                (count_in, recv_count),
                (response_in, response),
            )
        )
    ]
    for copy in loads:
        copy.start()

    barrier = pltpu.get_barrier_semaphore()

    def greet(device):
        pl.semaphore_signal(barrier, inc=1, device_id=device, device_id_type=MESH)

    after = (mp, lax.rem(space + 1, SPACE))
    before = (mp, lax.rem(space + SPACE - 1, SPACE))
    loop(1, 5, lambda i: greet(in_column(lax.rem(level + i, LEVELS))))
    loop(1, 5, lambda i: greet(in_column(lax.rem(level + LEVELS - i, LEVELS))))
    loop(1, PLANE, lambda i: greet(in_plane(lax.rem(place + i, PLANE))))
    greet(after)
    greet(before)

    low = iota((8, 128), 1) < 64
    lane = iota((1, 128), 1)
    for copy in loads[:4]:
        copy.wait()
    for c in range(8):
        work[c, 0:8, :] = jnp.ones((8, 128), F32)
        work[c, 72:80, :] = jnp.ones((8, 128), F32)

    @pl.when(magnetic)
    def _():
        b = work[6, 8:72, :]
        col = iota((64, 128), 1)
        right = jnp.where(col == 127, b, pltpu.roll(b, 127, 1))
        left = jnp.where(col == 0, b, pltpu.roll(b, 1, 1))
        current[...] = 0.5 * (right - left)

        def block(b):
            at = pl.ds(b * 16, 16)
            cells = cell[at, :]
            (got,) = pick(lambda r: (current[r : r + 1, :],), 64, cells >> 7, cells & 127, [jnp.zeros((16, 128), F32)])
            got = jnp.where(owner[at, :] == me, got, 0.0)
            for i in range(4):
                contribution[b * 4 + i] = got[i * 4 : i * 4 + 4]

        loop(0, 8, block)

    for c in range(8):
        for i in range(2):
            halo_out[0, i * 8 + c : i * 8 + c + 1, :] = work[c, 8 + i : 9 + i, :]
            halo_out[1, i * 8 + c : i * 8 + c + 1, :] = work[c, 70 + i : 71 + i, :]
    loads[4].wait()

    @pl.when(mp < 3)
    def _():
        points = src[...]
        turned = jnp.concatenate([points, points], axis=0).T
        index[...] = jnp.where(iota((64, 128), 1) < 64, turned[:64], turned[64:])

    def pack(half):
        def block(b):
            cells = index[pl.ds(half * 32 + b * 16, 16), :]
            got = pick(
                lambda r: tuple(work[c, 8 + r : 9 + r, :] for c in range(8)),
                64, cells >> 7, cells & 127, [jnp.zeros((16, 128), F32)] * 8,
            )
            for i in range(2):
                for q in range(4):
                    first = got[2 * q][i * 8 : i * 8 + 8]
                    second = got[2 * q + 1][i * 8 : i * 8 + 8]
                    outbox[half, b * 2 + i, :, q, :] = jnp.where(low, first, pltpu.roll(second, 64, 1))
                    outbox[half + 2, b * 2 + i, :, q, :] = jnp.where(low, pltpu.roll(first, 64, 1), second)

        loop(0, 2, block)

    halves = (lax.rem(x + 1, 2), lax.rem(x, 2))
    order = (halves[0], halves[0] + 2, lax.rem(x + 2, 4), x)

    def round_count(from_z):
        return jnp.where(from_z == 0, 2, jnp.where(from_z < 1 + ROUND, 1, 0))

    def depart(quarter):
        to_x = order[quarter]

        def one(i):
            push(
                outbox.at[to_x, i], mid.at[to_x, z], out_send, mid_recv.at[quarter // 2], in_column((mp + 1) * ZS + i)
            )

        loop(0, ZS - round_count(z), one)

    def depart_round(t):
        def one(i):
            below = in_column(lax.rem(level + LEVELS - 7, LEVELS))
            for quarter in (2 * t, 2 * t + 1):
                push(outbox.at[order[quarter], 3 - i], relay.at[i, quarter], out_send, relay_recv.at[t], below)

        loop(0, round_count(z), one)

    relays = [
        (jnp.logical_and(mp != 1, z == 1), pl.ds(0, 2)),
        (jnp.logical_and(mp != 1, jnp.logical_and(z >= 2, z < 2 + ROUND)), pl.ds(0, 1)),
    ]

    def pass_on(t):
        for here, slots in relays:

            @pl.when(here)
            def _(slots=slots):
                wait_for(relay.at[slots, pl.ds(2 * t, 2)], relay_recv.at[t])

                def one(i):
                    to = in_column(lax.rem(mp + 3, 4) * ZS + 3 - i)
                    for quarter in (2 * t, 2 * t + 1):
                        push(relay.at[i, quarter], mid.at[order[quarter], z - 1], relay_send, mid_recv.at[t], to)

                loop(0, slots.size, one)

    pl.semaphore_wait(barrier, 8 + PLANE - 1 + 2)
    for far in (4, LEVELS - 4):
        pl.semaphore_signal(
            known, inc=1, device_id=in_column(lax.rem(level + far, LEVELS)), device_id_type=MESH
        )

    @pl.when(magnetic)
    def _():
        def one(i):
            to = lax.rem(place + i, PLANE)
            push(contribution.at[to], rs.at[place], send.at[0], recv.at[0], in_plane(to))

        loop(PLANE // 2, PLANE, one)
        loop(1, PLANE // 2, one)
        rs[place] = contribution[place]

    push(halo_out.at[0], halo_in.at[1], halo_send.at[0], halo_recv.at[1], before)
    push(halo_out.at[1], halo_in.at[0], halo_send.at[1], halo_recv.at[0], after)

    @pl.when(mp < 3)
    def _():
        pack(halves[0])

    pl.semaphore_wait(known, 2)

    @pl.when(mp < 3)
    def _():
        depart_round(0)
        depart(0)
        pack(halves[1])

    @pl.when(magnetic)
    def _():
        wait_for(rs.at[pl.ds(0, PLANE - 1)], recv.at[0])
        total = rs[0]
        for i in range(1, PLANE):
            total = total + rs[i]
        part[...] = total

        def one(i):
            push(part, ar.at[level - 8], send.at[1], recv.at[1], in_column(lax.rem(level + i, LEVELS)))

        loop(8, LEVELS, one)
        loop(1, 8, one)
        ar[level - 8] = total

    loads[5].wait()
    loads[6].wait()

    @pl.when(mp > 0)
    def _():
        counts = recv_count[...]
        high = ((lane & 63) + 1).astype(F32)

        def used(b):
            return (iota((8, 128), 0) + b * 8) < counts

        slot_code[...] = invert(dst, used, lambda p: high, lambda p: ((lane >> 6) * 64 + p).astype(F32), 64).astype(I32)

    @pl.when(mp < 3)
    def _():
        depart_round(1)
        depart(1)
        depart(2)

    for i in range(2):
        wait_for(halo_in.at[i], halo_recv.at[i])
    for c in range(8):
        for i in range(2):
            work[c, 6 + i : 7 + i, :] = halo_in[0, i * 8 + c : i * 8 + c + 1, :]
            work[c, 72 + i : 73 + i, :] = halo_in[1, i * 8 + c : i * 8 + c + 1, :]
    for _ in range(2):
        sweep(work, 1, 1)
        sweep(work, 2, 0)

    @pl.when(magnetic)
    def _():
        wait_for(ar.at[pl.ds(0, 7)], recv.at[1])

    @pl.when(mp < 2)
    def _():
        wait_for(ar.at[pl.ds(0, 8)], recv.at[1])

    total = ar[0]
    for i in range(1, 8):
        total = total + ar[i]
    full[...] = total

    def give(i):
        push(full, spread.at[place], send.at[2], recv.at[2], in_plane(lax.rem(place + i, PLANE)))

    loop(PLANE // 2, PLANE, give)
    loop(1, PLANE // 2, give)
    spread[place] = total

    @pl.when(mp < 3)
    def _():
        depart(3)

    pass_on(0)

    @pl.when(magnetic)
    def _():
        def used(b):
            return owner[pl.ds(b * 8, 8), :] == me

        def high(i):
            row = lax.rem(lax.div(i, 8), 4) * 32 + lax.rem(i, 2) * 16 + lax.div(i, 32) + 1
            return (row + (lane >> 5) * 4).astype(F32)

        def low(i):
            return (lax.rem(lax.div(i, 2), 4) * 32 + (lane & 31)).astype(F32)

        iono_code[...] = invert(cell, used, high, low, 128).astype(I32)

    loads[7].wait()
    wait_for(spread.at[pl.ds(0, PLANE - 1)], recv.at[2])
    acc = jnp.zeros((32, 128), F32)
    for i in range(128):
        acc = acc + response[:, i * 128 : (i + 1) * 128].astype(F32) * spread[i // 4, i % 4 : i % 4 + 1, :]
    tile[...] = jnp.zeros_like(tile)
    tile[pl.ds(pl.multiple_of(z * 32, 32), 32), :] = acc
    line[...] = jnp.sum(tile[...].T, axis=0, keepdims=True)

    def report(i):
        push(line, lines.at[level], send.at[3], recv.at[3], in_column(8 + lax.rem(level + i, 8)))

    @pl.when(magnetic)
    def _():
        loop(1, 8, report)
        lines[level] = line[...]

    @pl.when(mp < 2)
    def _():
        loop(0, 8, report)

    def forward(to_x, t, first):
        def one(i):
            to = lax.rem(yc + i, YC)
            push(mid.at[to_x, :, to], inbox.at[x, :, yc], fwd_send.at[t], inbox_recv.at[t], in_plane(to_x * YC + to))

        loop(first, YC, one)

    pass_on(1)

    @pl.when(mp > 0)
    def _():
        wait_for(mid.at[pl.ds(0, 2)], mid_recv.at[0])
        forward(order[0], 0, 0)
        forward(order[1], 0, 0)

    @pl.when(magnetic)
    def _():
        wait_for(lines.at[pl.ds(0, LEVELS - 1)], recv.at[3])
        rows = []
        for m in range(4):
            row = lines[m * 4]
            for i in range(1, 4):
                row = row + lines[m * 4 + i]
            rows.append(row)
        mine = jnp.concatenate(rows, axis=0)
        pot_part[...] = mine

        def one(i):
            push(pot_part, pot.at[place], send.at[4], recv.at[4], in_plane(lax.rem(place + i, PLANE)))

        loop(PLANE // 2, PLANE, one)
        loop(1, PLANE // 2, one)
        pot[place] = mine

    def unpack(half):
        for i in range(4):
            for q in range(4):
                first = inbox[half, i, :, q, :]
                second = inbox[half + 2, i, :, q, :]
                table[2 * q, i * 8 : i * 8 + 8, :] = jnp.where(low, first, pltpu.roll(second, 64, 1))
                table[2 * q + 1, i * 8 : i * 8 + 8, :] = jnp.where(low, pltpu.roll(first, 64, 1), second)

        def block(b):
            at = pl.ds(pl.multiple_of(8 + b * 16, 8), 16)
            row = slot_code[pl.ds(b * 16, 16), :] - (1 + half * 32)
            spot = slot_code[pl.ds(64 + b * 16, 16), :]
            got = pick(
                lambda r: tuple(table[c, r : r + 1, :] for c in range(8)),
                32, row, spot, [work[c, at, :] for c in range(8)],
            )
            for c in range(8):
                work[c, at, :] = got[c]

        loop(0, 4, block)

    @pl.when(mp > 0)
    def _():
        wait_for(mid.at[pl.ds(0, 2)], mid_recv.at[1])
        forward(order[2], 1, 0)
        forward(order[3], 1, 1)
        inbox[x, :, yc] = mid[x, :, yc]
        wait_for(inbox.at[pl.ds(0, 2)], inbox_recv.at[0])
        unpack(halves[0])
        wait_for(inbox.at[pl.ds(0, 3), :, pl.ds(0, 5)], inbox_recv.at[1])
        unpack(halves[1])

    @pl.when(magnetic)
    def _():
        wait_for(pot.at[pl.ds(0, PLANE - 1)], recv.at[4])

        def block(b):
            at = pl.ds(pl.multiple_of(8 + b * 16, 8), 16)
            row = iono_code[pl.ds(b * 16, 16), :] - 1
            spot = iono_code[pl.ds(64 + b * 16, 16), :]
            (got,) = pick(
                lambda r: (pot[r // 4, r % 4 : r % 4 + 1, :],), 128, row, spot, [jnp.zeros((16, 128), F32)]
            )
            work[1, at, :] = work[1, at, :] + 0.5 * work[0, at, :] * got

        loop(0, 4, block)

    state_out[...] = work[:, 8:72, :]

    for i in range(2):
        wait_for(halo_out.at[i], halo_send.at[i])
    wait_for(spread.at[pl.ds(0, PLANE - 1)], send.at[2])

    @pl.when(mp < 3)
    def _():
        wait_for(mid, out_send)

    for here, slots in relays:

        @pl.when(here)
        def _(slots=slots):
            wait_for(relay.at[slots], relay_send)

    @pl.when(mp > 0)
    def _():
        wait_for(inbox.at[pl.ds(0, 2)], fwd_send.at[0])
        wait_for(inbox.at[pl.ds(0, 3), :, pl.ds(0, 5)], fwd_send.at[1])

    @pl.when(magnetic)
    def _():
        wait_for(rs.at[pl.ds(0, PLANE - 1)], send.at[0])
        wait_for(ar.at[pl.ds(0, LEVELS - 1)], send.at[1])
        wait_for(lines.at[pl.ds(0, 7)], send.at[3])
        wait_for(pot.at[pl.ds(0, PLANE - 1)], send.at[4])

    @pl.when(mp < 2)
    def _():
        wait_for(lines.at[pl.ds(0, 8)], send.at[3])


def hand_out(state, density_out, fields_out, sem):
    copies = [
        pltpu.make_async_copy(state.at[0], density_out.at[0], sem.at[0]),
        pltpu.make_async_copy(state.at[pl.ds(1, 7)], fields_out.at[0], sem.at[1]),
    ]
    for copy in copies:
        copy.start()
    for copy in copies:
        copy.wait()


def local(density, fields, src_points, dst_points, recv_count, iono_owner, iono_cell, response):
    vmem = pltpu.VMEM
    dma = pltpu.SemaphoreType.DMA
    hbm = pl.BlockSpec(memory_space=pl.ANY)
    state = pl.pallas_call(
        cycle_kernel,
        out_shape=vmem((8, 64, 128), F32),
        in_specs=[hbm] * 8,
        out_specs=pl.BlockSpec(memory_space=vmem),
        scratch_shapes=[
            vmem((8, 80, 128), F32),
            vmem((64, 128), I32),
            vmem((64, 128), I32),
            vmem((1, 128), I32),
            vmem((128, 128), I32),
            vmem((128, 128), I32),
            vmem((32, 16384), BF16),
            vmem((64, 128), I32),
            vmem((64, 128), F32),
            vmem((2, 16, 128), F32),
            vmem((2, 16, 128), F32),
            vmem((4, ZS, YC, 4, 128), F32),
            vmem((4, ZS, YC, 4, 128), F32),
            vmem((4, ZS, YC, 4, 128), F32),
            vmem((2, 4, YC, 4, 128), F32),
            vmem((8, 32, 128), F32),
            vmem((PLANE, 4, 128), F32),
            vmem((PLANE, 4, 128), F32),
            vmem((4, 128), F32),
            vmem((LEVELS, 4, 128), F32),
            vmem((4, 128), F32),
            vmem((PLANE, 4, 128), F32),
            vmem((128, 128), F32),
            vmem((1, 128), F32),
            vmem((LEVELS, 1, 128), F32),
            vmem((4, 128), F32),
            vmem((PLANE, 4, 128), F32),
            vmem((128, 128), I32),
            vmem((128, 128), I32),
            dma((8,)),
            dma((2,)),
            dma((2,)),
            dma((5,)),
            dma((5,)),
            dma,
            dma((2,)),
            dma((2,)),
            dma((2,)),
            dma,
            dma((2,)),
            pltpu.SemaphoreType.REGULAR,
        ],
        compiler_params=pltpu.CompilerParams(
            collective_id=0, has_side_effects=True, vmem_limit_bytes=56 * 1024 * 1024
        ),
        name="cycle",
    )(
        density, fields, src_points[0, 0].T, dst_points[0, 0].T, recv_count[0],
        iono_owner.reshape(128, 128), iono_cell.reshape(128, 128), response,
    )
    return state[:1], state[1:][None]


def solution(mesh):
    placed = (
        P("mp", "space", None),
        P("mp", None, "space", None),
        P("mp", "space", None, None),
        P("mp", "space", None, None),
        P("mp", "space", None),
        P(),
        P(),
        P(("mp", "space"), None),
    )
    return jax.shard_map(
        local,
        mesh=mesh,
        in_specs=placed,
        out_specs=(P("mp", "space", None), P("mp", None, "space", None)),
        check_vma=False,
    )
```

```python
import jax
import jax.numpy as jnp
from jax import lax
from jax.experimental import pallas as pl
from jax.experimental.pallas import tpu as pltpu
from jax.sharding import PartitionSpec as P

MESH = pl.DeviceIdType.MESH
YC = 8
ZS = 4
SPACE = 128
PLANE = 32
LEVELS = 16
ROUND = 2
LAMBDA_STEP = 0.1
F32 = jnp.float32
I32 = jnp.int32
BF16 = jnp.bfloat16


def iota(shape, dim):
    return lax.broadcasted_iota(I32, shape, dim)


def loop(first, last, body):
    def step(i, carry):
        body(i)
        return carry

    lax.fori_loop(first, last, step, 0)


def wait_for(ref, sem):
    pltpu.make_async_copy(ref, ref, sem).wait()


def push(src_ref, dst_ref, send_sem, recv_sem, device):
    pltpu.make_async_remote_copy(
        src_ref=src_ref,
        dst_ref=dst_ref,
        send_sem=send_sem,
        recv_sem=recv_sem,
        device_id=device,
        device_id_type=MESH,
    ).start()


def pick(lines, count, row, lane, held):
    shape = row.shape
    for r in range(count):
        hit = row == r
        held = [
            jnp.where(
                hit,
                jnp.take_along_axis(jnp.broadcast_to(line, shape), lane, axis=1, mode="promise_in_bounds"),
                old,
            )
            for line, old in zip(lines(r), held)
        ]
    return held


def invert(rows_ref, used, high_of, low_of, count):
    def step(b, total):
        cells = rows_ref[pl.ds(b * 8, 8), :]
        row8 = jnp.where(used(b), cells >> 7, -1)
        col8 = cells & 127
        left, right = [], []
        for s in range(8):
            hit = iota((64, 128), 0) == row8[s : s + 1]
            left.append(
                jnp.concatenate(
                    [jnp.where(hit, high_of(b * 8 + s), 0.0), jnp.where(hit, low_of(b * 8 + s), 0.0)], axis=0
                ).astype(BF16)
            )
            right.append(jnp.where(iota((128, 128), 0) == col8[s : s + 1], 1.0, 0.0).astype(BF16))
        return total + lax.dot_general(
            jnp.concatenate(left, axis=1),
            jnp.concatenate(right, axis=1),
            (((1,), (1,)), ((), ())),
            preferred_element_type=F32,
        )

    return lax.fori_loop(0, count // 8, step, jnp.zeros((128, 128), F32))


def sweep(work, speed, axis):
    shape = (80, 128)
    size = shape[axis]
    at = iota(shape, axis)

    def above(value):
        moved = pltpu.roll(value, size - 1, axis)
        return jnp.where(at == size - 1, value, moved) if axis == 1 else moved

    u = work[speed] / work[0]
    u_up = above(u)
    fast = 0.5 * (jnp.maximum(jnp.abs(u), jnp.abs(u_up)) + 1.0)
    for c in range(8):
        q = work[c]
        flux = u * q
        face = 0.5 * (flux + above(flux)) - fast * (above(q) - q)
        below = pltpu.roll(face, 1, axis)
        if axis == 1:
            below = jnp.where(at == 0, flux, below)
        work[c] = q - LAMBDA_STEP * (face - below)


def cycle_kernel(
    density_in, fields_in, src_in, dst_in, count_in, owner_in, cell_in, response_in,
    state_out,
    work, src, dst, recv_count, owner, cell, response, index, current, halo_out, halo_in,
    outbox, mid, inbox, relay, table, contribution, rs, part, ar, full, spread, tile, line, lines, pot_part, pot,
    slot_code, iono_code,
    load, halo_send, halo_recv, send, recv, out_send, mid_recv, fwd_send, inbox_recv, relay_send, relay_recv, known,
):
    mp = lax.axis_index("mp")
    space = lax.axis_index("space")
    x = lax.div(space, ZS * YC)
    z = lax.rem(lax.div(space, YC), ZS)
    yc = lax.rem(space, YC)
    place = x * YC + yc
    level = mp * ZS + z
    magnetic = mp >= 2
    me = (mp - 2) * SPACE + space

    def in_plane(p):
        return (mp, (lax.div(p, YC) * ZS + z) * YC + lax.rem(p, YC))

    def elsewhere_in_plane(body):
        steps = sorted(
            ((dx, dy) for dx in range(4) for dy in range(4)),
            key=lambda d: -(min(d[0], 4 - d[0]) + min(d[1], 4 - d[1])),
        )
        core = lax.rem(yc, 2)
        for dx, dy in steps:
            chip = lax.rem(x + dx, 4) * YC + lax.rem(lax.div(yc, 2) + dy, 4) * 2
            if dx or dy:
                body(chip + core)
            body(chip + 1 - core)

    def in_column(l):
        return (lax.div(l, ZS), (x * ZS + lax.rem(l, ZS)) * YC + yc)

    body = pl.ds(8, 64)
    loads = [
        pltpu.make_async_copy(a, b, load.at[i])
        for i, (a, b) in enumerate(
            (
                (fields_in.at[0], work.at[pl.ds(1, 7), body]),
                (density_in.at[0], work.at[0, body]),
                (cell_in, cell),
                (owner_in, owner),
                (src_in, src),
                (dst_in, dst),
                (count_in, recv_count),
                (response_in, response),
            )
        )
    ]
    for copy in loads:
        copy.start()

    barrier = pltpu.get_barrier_semaphore()

    def greet(device):
        pl.semaphore_signal(barrier, inc=1, device_id=device, device_id_type=MESH)

    after = (mp, lax.rem(space + 1, SPACE))
    before = (mp, lax.rem(space + SPACE - 1, SPACE))
    greet(after)
    greet(before)
    for i in (4, 3):
        greet(in_column(lax.rem(level + i, LEVELS)))
        greet(in_column(lax.rem(level + LEVELS - i, LEVELS)))
    elsewhere_in_plane(lambda p: greet(in_plane(p)))
    for i in (2, 1):
        greet(in_column(lax.rem(level + i, LEVELS)))
        greet(in_column(lax.rem(level + LEVELS - i, LEVELS)))

    low = iota((8, 128), 1) < 64
    lane = iota((1, 128), 1)
    for copy in loads[:4]:
        copy.wait()
    for c in range(8):
        work[c, 0:8, :] = jnp.ones((8, 128), F32)
        work[c, 72:80, :] = jnp.ones((8, 128), F32)

    @pl.when(magnetic)
    def _():
        b = work[6, 8:72, :]
        col = iota((64, 128), 1)
        right = jnp.where(col == 127, b, pltpu.roll(b, 127, 1))
        left = jnp.where(col == 0, b, pltpu.roll(b, 1, 1))
        current[...] = 0.5 * (right - left)

        def block(b):
            at = pl.ds(b * 16, 16)
            cells = cell[at, :]
            (got,) = pick(lambda r: (current[r : r + 1, :],), 64, cells >> 7, cells & 127, [jnp.zeros((16, 128), F32)])
            got = jnp.where(owner[at, :] == me, got, 0.0)
            for i in range(4):
                contribution[b * 4 + i] = got[i * 4 : i * 4 + 4]

        loop(0, 8, block)

    for c in range(8):
        for i in range(2):
            halo_out[0, i * 8 + c : i * 8 + c + 1, :] = work[c, 8 + i : 9 + i, :]
            halo_out[1, i * 8 + c : i * 8 + c + 1, :] = work[c, 70 + i : 71 + i, :]
    loads[4].wait()

    @pl.when(mp < 3)
    def _():
        points = src[...]
        turned = jnp.concatenate([points, points], axis=0).T
        index[...] = jnp.where(iota((64, 128), 1) < 64, turned[:64], turned[64:])

    def pack(half):
        def block(b):
            cells = index[pl.ds(half * 32 + b * 16, 16), :]
            got = pick(
                lambda r: tuple(work[c, 8 + r : 9 + r, :] for c in range(8)),
                64, cells >> 7, cells & 127, [jnp.zeros((16, 128), F32)] * 8,
            )
            for i in range(2):
                for q in range(4):
                    first = got[2 * q][i * 8 : i * 8 + 8]
                    second = got[2 * q + 1][i * 8 : i * 8 + 8]
                    outbox[half, b * 2 + i, :, q, :] = jnp.where(low, first, pltpu.roll(second, 64, 1))
                    outbox[half + 2, b * 2 + i, :, q, :] = jnp.where(low, pltpu.roll(first, 64, 1), second)

        loop(0, 2, block)

    halves = (lax.rem(x + 1, 2), lax.rem(x, 2))
    order = (halves[0], halves[0] + 2, lax.rem(x + 2, 4), x)

    def round_count(from_z):
        return jnp.where(from_z == 0, 2, jnp.where(from_z < 1 + ROUND, 1, 0))

    def depart(quarter):
        to_x = order[quarter]

        def one(i):
            push(
                outbox.at[to_x, i], mid.at[to_x, z], out_send, mid_recv.at[quarter // 2], in_column((mp + 1) * ZS + i)
            )

        loop(0, ZS - round_count(z), one)

    def depart_round(t):
        def one(i):
            below = in_column(lax.rem(level + LEVELS - 7, LEVELS))
            for quarter in (2 * t, 2 * t + 1):
                push(outbox.at[order[quarter], 3 - i], relay.at[i, quarter], out_send, relay_recv.at[t], below)

        loop(0, round_count(z), one)

    relays = [
        (jnp.logical_and(mp != 1, z == 1), pl.ds(0, 2)),
        (jnp.logical_and(mp != 1, jnp.logical_and(z >= 2, z < 2 + ROUND)), pl.ds(0, 1)),
    ]

    def pass_on(t):
        for here, slots in relays:

            @pl.when(here)
            def _(slots=slots):
                wait_for(relay.at[slots, pl.ds(2 * t, 2)], relay_recv.at[t])

                def one(i):
                    to = in_column(lax.rem(mp + 3, 4) * ZS + 3 - i)
                    for quarter in (2 * t, 2 * t + 1):
                        push(relay.at[i, quarter], mid.at[order[quarter], z - 1], relay_send, mid_recv.at[t], to)

                loop(0, slots.size, one)

    pl.semaphore_wait(barrier, 8 + PLANE - 1 + 2)
    for far in (4, LEVELS - 4):
        pl.semaphore_signal(
            known, inc=1, device_id=in_column(lax.rem(level + far, LEVELS)), device_id_type=MESH
        )

    @pl.when(magnetic)
    def _():
        elsewhere_in_plane(
            lambda p: push(contribution.at[p], rs.at[place], send.at[0], recv.at[0], in_plane(p))
        )
        rs[place] = contribution[place]

    push(halo_out.at[0], halo_in.at[1], halo_send.at[0], halo_recv.at[1], before)
    push(halo_out.at[1], halo_in.at[0], halo_send.at[1], halo_recv.at[0], after)

    @pl.when(mp < 3)
    def _():
        pack(halves[0])

    pl.semaphore_wait(known, 2)

    @pl.when(mp < 3)
    def _():
        depart_round(0)
        depart(0)
        pack(halves[1])

    @pl.when(magnetic)
    def _():
        wait_for(rs.at[pl.ds(0, PLANE - 1)], recv.at[0])
        total = rs[0]
        for i in range(1, PLANE):
            total = total + rs[i]
        part[...] = total

        for i in (8, 7, 9, 6, 10, 5, 11, 4, 12, 3, 13, 2, 14, 1, 15):
            push(part, ar.at[level - 8], send.at[1], recv.at[1], in_column(lax.rem(level + i, LEVELS)))
        ar[level - 8] = total

    loads[5].wait()
    loads[6].wait()

    @pl.when(mp > 0)
    def _():
        counts = recv_count[...]
        high = ((lane & 63) + 1).astype(F32)

        def used(b):
            return (iota((8, 128), 0) + b * 8) < counts

        slot_code[...] = invert(dst, used, lambda p: high, lambda p: ((lane >> 6) * 64 + p).astype(F32), 64).astype(I32)

    @pl.when(mp < 3)
    def _():
        depart_round(1)
        depart(1)
        depart(2)

    for i in range(2):
        wait_for(halo_in.at[i], halo_recv.at[i])
    for c in range(8):
        for i in range(2):
            work[c, 6 + i : 7 + i, :] = halo_in[0, i * 8 + c : i * 8 + c + 1, :]
            work[c, 72 + i : 73 + i, :] = halo_in[1, i * 8 + c : i * 8 + c + 1, :]
    for _ in range(2):
        sweep(work, 1, 1)
        sweep(work, 2, 0)

    @pl.when(magnetic)
    def _():
        wait_for(ar.at[pl.ds(0, 7)], recv.at[1])

    @pl.when(mp < 2)
    def _():
        wait_for(ar.at[pl.ds(0, 8)], recv.at[1])

    total = ar[0]
    for i in range(1, 8):
        total = total + ar[i]
    full[...] = total

    elsewhere_in_plane(lambda p: push(full, spread.at[place], send.at[2], recv.at[2], in_plane(p)))
    spread[place] = total

    @pl.when(mp < 3)
    def _():
        depart(3)

    pass_on(0)

    @pl.when(magnetic)
    def _():
        def used(b):
            return owner[pl.ds(b * 8, 8), :] == me

        def high(i):
            row = lax.rem(lax.div(i, 8), 4) * 32 + lax.rem(i, 2) * 16 + lax.div(i, 32) + 1
            return (row + (lane >> 5) * 4).astype(F32)

        def low(i):
            return (lax.rem(lax.div(i, 2), 4) * 32 + (lane & 31)).astype(F32)

        iono_code[...] = invert(cell, used, high, low, 128).astype(I32)

    loads[7].wait()
    wait_for(spread.at[pl.ds(0, PLANE - 1)], recv.at[2])
    acc = jnp.zeros((32, 128), F32)
    for i in range(128):
        acc = acc + response[:, i * 128 : (i + 1) * 128].astype(F32) * spread[i // 4, i % 4 : i % 4 + 1, :]
    tile[...] = jnp.zeros_like(tile)
    tile[pl.ds(pl.multiple_of(z * 32, 32), 32), :] = acc
    line[...] = jnp.sum(tile[...].T, axis=0, keepdims=True)

    def report(i):
        push(line, lines.at[level], send.at[3], recv.at[3], in_column(8 + lax.rem(level + i, 8)))

    @pl.when(magnetic)
    def _():
        loop(1, 8, report)
        lines[level] = line[...]

    @pl.when(mp < 2)
    def _():
        loop(0, 8, report)

    def forward(to_x, t, first):
        core = lax.rem(yc, 2)
        for dy in (2, 1, 3, 0):
            for dc in (0, 1):
                if first and dy + dc == 0:
                    continue
                to = lax.rem(lax.div(yc, 2) + dy, 4) * 2 + lax.rem(core + dc, 2)
                push(
                    mid.at[to_x, :, to], inbox.at[x, :, yc], fwd_send.at[t], inbox_recv.at[t], in_plane(to_x * YC + to)
                )

    pass_on(1)

    @pl.when(mp > 0)
    def _():
        wait_for(mid.at[pl.ds(0, 2)], mid_recv.at[0])
        forward(order[0], 0, 0)
        forward(order[1], 0, 0)

    @pl.when(magnetic)
    def _():
        wait_for(lines.at[pl.ds(0, LEVELS - 1)], recv.at[3])
        rows = []
        for m in range(4):
            row = lines[m * 4]
            for i in range(1, 4):
                row = row + lines[m * 4 + i]
            rows.append(row)
        mine = jnp.concatenate(rows, axis=0)
        pot_part[...] = mine

        elsewhere_in_plane(lambda p: push(pot_part, pot.at[place], send.at[4], recv.at[4], in_plane(p)))
        pot[place] = mine

    def unpack(half):
        for i in range(4):
            for q in range(4):
                first = inbox[half, i, :, q, :]
                second = inbox[half + 2, i, :, q, :]
                table[2 * q, i * 8 : i * 8 + 8, :] = jnp.where(low, first, pltpu.roll(second, 64, 1))
                table[2 * q + 1, i * 8 : i * 8 + 8, :] = jnp.where(low, pltpu.roll(first, 64, 1), second)

        def block(b):
            at = pl.ds(pl.multiple_of(8 + b * 16, 8), 16)
            row = slot_code[pl.ds(b * 16, 16), :] - (1 + half * 32)
            spot = slot_code[pl.ds(64 + b * 16, 16), :]
            got = pick(
                lambda r: tuple(table[c, r : r + 1, :] for c in range(8)),
                32, row, spot, [work[c, at, :] for c in range(8)],
            )
            for c in range(8):
                work[c, at, :] = got[c]

        loop(0, 4, block)

    @pl.when(mp > 0)
    def _():
        wait_for(mid.at[pl.ds(0, 2)], mid_recv.at[1])
        forward(order[2], 1, 0)
        forward(order[3], 1, 1)
        inbox[x, :, yc] = mid[x, :, yc]
        wait_for(inbox.at[pl.ds(0, 2)], inbox_recv.at[0])
        unpack(halves[0])
        wait_for(inbox.at[pl.ds(0, 3), :, pl.ds(0, 5)], inbox_recv.at[1])
        unpack(halves[1])

    @pl.when(magnetic)
    def _():
        wait_for(pot.at[pl.ds(0, PLANE - 1)], recv.at[4])

        def block(b):
            at = pl.ds(pl.multiple_of(8 + b * 16, 8), 16)
            row = iono_code[pl.ds(b * 16, 16), :] - 1
            spot = iono_code[pl.ds(64 + b * 16, 16), :]
            (got,) = pick(
                lambda r: (pot[r // 4, r % 4 : r % 4 + 1, :],), 128, row, spot, [jnp.zeros((16, 128), F32)]
            )
            work[1, at, :] = work[1, at, :] + 0.5 * work[0, at, :] * got

        loop(0, 4, block)

    state_out[...] = work[:, 8:72, :]

    for i in range(2):
        wait_for(halo_out.at[i], halo_send.at[i])
    wait_for(spread.at[pl.ds(0, PLANE - 1)], send.at[2])

    @pl.when(mp < 3)
    def _():
        wait_for(mid, out_send)

    for here, slots in relays:

        @pl.when(here)
        def _(slots=slots):
            wait_for(relay.at[slots], relay_send)

    @pl.when(mp > 0)
    def _():
        wait_for(inbox.at[pl.ds(0, 2)], fwd_send.at[0])
        wait_for(inbox.at[pl.ds(0, 3), :, pl.ds(0, 5)], fwd_send.at[1])

    @pl.when(magnetic)
    def _():
        wait_for(rs.at[pl.ds(0, PLANE - 1)], send.at[0])
        wait_for(ar.at[pl.ds(0, LEVELS - 1)], send.at[1])
        wait_for(lines.at[pl.ds(0, 7)], send.at[3])
        wait_for(pot.at[pl.ds(0, PLANE - 1)], send.at[4])

    @pl.when(mp < 2)
    def _():
        wait_for(lines.at[pl.ds(0, 8)], send.at[3])


def hand_out(state, density_out, fields_out, sem):
    copies = [
        pltpu.make_async_copy(state.at[0], density_out.at[0], sem.at[0]),
        pltpu.make_async_copy(state.at[pl.ds(1, 7)], fields_out.at[0], sem.at[1]),
    ]
    for copy in copies:
        copy.start()
    for copy in copies:
        copy.wait()


def local(density, fields, src_points, dst_points, recv_count, iono_owner, iono_cell, response):
    vmem = pltpu.VMEM
    dma = pltpu.SemaphoreType.DMA
    hbm = pl.BlockSpec(memory_space=pl.ANY)
    state = pl.pallas_call(
        cycle_kernel,
        out_shape=vmem((8, 64, 128), F32),
        in_specs=[hbm] * 8,
        out_specs=pl.BlockSpec(memory_space=vmem),
        scratch_shapes=[
            vmem((8, 80, 128), F32),
            vmem((64, 128), I32),
            vmem((64, 128), I32),
            vmem((1, 128), I32),
            vmem((128, 128), I32),
            vmem((128, 128), I32),
            vmem((32, 16384), BF16),
            vmem((64, 128), I32),
            vmem((64, 128), F32),
            vmem((2, 16, 128), F32),
            vmem((2, 16, 128), F32),
            vmem((4, ZS, YC, 4, 128), F32),
            vmem((4, ZS, YC, 4, 128), F32),
            vmem((4, ZS, YC, 4, 128), F32),
            vmem((2, 4, YC, 4, 128), F32),
            vmem((8, 32, 128), F32),
            vmem((PLANE, 4, 128), F32),
            vmem((PLANE, 4, 128), F32),
            vmem((4, 128), F32),
            vmem((LEVELS, 4, 128), F32),
            vmem((4, 128), F32),
            vmem((PLANE, 4, 128), F32),
            vmem((128, 128), F32),
            vmem((1, 128), F32),
            vmem((LEVELS, 1, 128), F32),
            vmem((4, 128), F32),
            vmem((PLANE, 4, 128), F32),
            vmem((128, 128), I32),
            vmem((128, 128), I32),
            dma((8,)),
            dma((2,)),
            dma((2,)),
            dma((5,)),
            dma((5,)),
            dma,
            dma((2,)),
            dma((2,)),
            dma((2,)),
            dma,
            dma((2,)),
            pltpu.SemaphoreType.REGULAR,
        ],
        compiler_params=pltpu.CompilerParams(
            collective_id=0, has_side_effects=True, vmem_limit_bytes=56 * 1024 * 1024
        ),
        name="cycle",
    )(
        density, fields, src_points[0, 0].T, dst_points[0, 0].T, recv_count[0],
        iono_owner.reshape(128, 128), iono_cell.reshape(128, 128), response,
    )
    return state[:1], state[1:][None]


def solution(mesh):
    placed = (
        P("mp", "space", None),
        P("mp", None, "space", None),
        P("mp", "space", None, None),
        P("mp", "space", None, None),
        P("mp", "space", None),
        P(),
        P(),
        P(("mp", "space"), None),
    )
    return jax.shard_map(
        local,
        mesh=mesh,
        in_specs=placed,
        out_specs=(P("mp", "space", None), P("mp", None, "space", None)),
        check_vma=False,
    )
```

```python
import jax
import jax.numpy as jnp
from jax import lax
from jax.experimental import pallas as pl
from jax.experimental.pallas import tpu as pltpu
from jax.sharding import PartitionSpec as P

MESH = pl.DeviceIdType.MESH
YC = 8
ZS = 4
SPACE = 128
PLANE = 32
LEVELS = 16
ROUND = 2
LAMBDA_STEP = 0.1
F32 = jnp.float32
I32 = jnp.int32
BF16 = jnp.bfloat16


def iota(shape, dim):
    return lax.broadcasted_iota(I32, shape, dim)


def loop(first, last, body):
    def step(i, carry):
        body(i)
        return carry

    lax.fori_loop(first, last, step, 0)


def wait_for(ref, sem):
    pltpu.make_async_copy(ref, ref, sem).wait()


def push(src_ref, dst_ref, send_sem, recv_sem, device):
    pltpu.make_async_remote_copy(
        src_ref=src_ref,
        dst_ref=dst_ref,
        send_sem=send_sem,
        recv_sem=recv_sem,
        device_id=device,
        device_id_type=MESH,
    ).start()


def pick(lines, count, row, lane, held):
    shape = row.shape
    for r in range(count):
        hit = row == r
        held = [
            jnp.where(
                hit,
                jnp.take_along_axis(jnp.broadcast_to(line, shape), lane, axis=1, mode="promise_in_bounds"),
                old,
            )
            for line, old in zip(lines(r), held)
        ]
    return held


def invert(rows_ref, used, high_of, low_of, count):
    def step(b, total):
        cells = rows_ref[pl.ds(b * 8, 8), :]
        row8 = jnp.where(used(b), cells >> 7, -1)
        col8 = cells & 127
        left, right = [], []
        for s in range(8):
            hit = iota((64, 128), 0) == row8[s : s + 1]
            left.append(
                jnp.concatenate(
                    [jnp.where(hit, high_of(b * 8 + s), 0.0), jnp.where(hit, low_of(b * 8 + s), 0.0)], axis=0
                ).astype(BF16)
            )
            right.append(jnp.where(iota((128, 128), 0) == col8[s : s + 1], 1.0, 0.0).astype(BF16))
        return total + lax.dot_general(
            jnp.concatenate(left, axis=1),
            jnp.concatenate(right, axis=1),
            (((1,), (1,)), ((), ())),
            preferred_element_type=F32,
        )

    return lax.fori_loop(0, count // 8, step, jnp.zeros((128, 128), F32))


def sweep(work, speed, axis):
    shape = (80, 128)
    size = shape[axis]
    at = iota(shape, axis)

    def above(value):
        moved = pltpu.roll(value, size - 1, axis)
        return jnp.where(at == size - 1, value, moved) if axis == 1 else moved

    u = work[speed] / work[0]
    u_up = above(u)
    fast = 0.5 * (jnp.maximum(jnp.abs(u), jnp.abs(u_up)) + 1.0)
    for c in range(8):
        q = work[c]
        flux = u * q
        face = 0.5 * (flux + above(flux)) - fast * (above(q) - q)
        below = pltpu.roll(face, 1, axis)
        if axis == 1:
            below = jnp.where(at == 0, flux, below)
        work[c] = q - LAMBDA_STEP * (face - below)


def cycle_kernel(
    density_in, fields_in, src_in, dst_in, count_in, owner_in, cell_in, response_in,
    state_out,
    work, src, dst, recv_count, owner, cell, response, index, current, halo_out, halo_in,
    outbox, mid, inbox, relay, table, contribution, rs, part, ar, full, spread, tile, line, lines, pot_part, pot,
    slot_code, iono_code,
    load, halo_send, halo_recv, send, recv, out_send, mid_recv, fwd_send, inbox_recv, relay_send, relay_recv, known,
):
    mp = lax.axis_index("mp")
    space = lax.axis_index("space")
    x = lax.div(space, ZS * YC)
    z = lax.rem(lax.div(space, YC), ZS)
    yc = lax.rem(space, YC)
    place = x * YC + yc
    level = mp * ZS + z
    magnetic = mp >= 2
    me = (mp - 2) * SPACE + space

    def in_plane(p):
        return (mp, (lax.div(p, YC) * ZS + z) * YC + lax.rem(p, YC))

    def elsewhere_in_plane(body):
        steps = sorted(
            ((dx, dy) for dx in range(4) for dy in range(4)),
            key=lambda d: -(min(d[0], 4 - d[0]) + min(d[1], 4 - d[1])),
        )
        core = lax.rem(yc, 2)
        for dx, dy in steps:
            chip = lax.rem(x + dx, 4) * YC + lax.rem(lax.div(yc, 2) + dy, 4) * 2
            if dx or dy:
                body(chip + core)
            body(chip + 1 - core)

    def in_column(l):
        return (lax.div(l, ZS), (x * ZS + lax.rem(l, ZS)) * YC + yc)

    body = pl.ds(8, 64)
    loads = [
        pltpu.make_async_copy(a, b, load.at[i])
        for i, (a, b) in enumerate(
            (
                (fields_in.at[0], work.at[pl.ds(1, 7), body]),
                (density_in.at[0], work.at[0, body]),
                (cell_in, cell),
                (owner_in, owner),
                (src_in, src),
                (dst_in, dst),
                (count_in, recv_count),
                (response_in, response),
            )
        )
    ]
    for copy in loads:
        copy.start()

    barrier = pltpu.get_barrier_semaphore()

    def greet(device):
        pl.semaphore_signal(barrier, inc=1, device_id=device, device_id_type=MESH)

    after = (mp, lax.rem(space + 1, SPACE))
    before = (mp, lax.rem(space + SPACE - 1, SPACE))
    greet(after)
    greet(before)
    for i in (4, 3):
        greet(in_column(lax.rem(level + i, LEVELS)))
        greet(in_column(lax.rem(level + LEVELS - i, LEVELS)))
    elsewhere_in_plane(lambda p: greet(in_plane(p)))
    for i in (2, 1):
        greet(in_column(lax.rem(level + i, LEVELS)))
        greet(in_column(lax.rem(level + LEVELS - i, LEVELS)))

    low = iota((8, 128), 1) < 64
    lane = iota((1, 128), 1)
    for copy in loads[:4]:
        copy.wait()
    for c in range(8):
        work[c, 0:8, :] = jnp.ones((8, 128), F32)
        work[c, 72:80, :] = jnp.ones((8, 128), F32)

    @pl.when(magnetic)
    def _():
        b = work[6, 8:72, :]
        col = iota((64, 128), 1)
        right = jnp.where(col == 127, b, pltpu.roll(b, 127, 1))
        left = jnp.where(col == 0, b, pltpu.roll(b, 1, 1))
        current[...] = 0.5 * (right - left)

        def block(b):
            at = pl.ds(b * 16, 16)
            cells = cell[at, :]
            (got,) = pick(lambda r: (current[r : r + 1, :],), 64, cells >> 7, cells & 127, [jnp.zeros((16, 128), F32)])
            got = jnp.where(owner[at, :] == me, got, 0.0)
            for i in range(4):
                contribution[b * 4 + i] = got[i * 4 : i * 4 + 4]

        loop(0, 8, block)

    for c in range(8):
        for i in range(2):
            halo_out[0, i * 8 + c : i * 8 + c + 1, :] = work[c, 8 + i : 9 + i, :]
            halo_out[1, i * 8 + c : i * 8 + c + 1, :] = work[c, 70 + i : 71 + i, :]
    loads[4].wait()

    @pl.when(mp < 3)
    def _():
        points = src[...]
        turned = jnp.concatenate([points, points], axis=0).T
        index[...] = jnp.where(iota((64, 128), 1) < 64, turned[:64], turned[64:])

    def pack(half):
        def block(b):
            cells = index[pl.ds(half * 32 + b * 16, 16), :]
            got = pick(
                lambda r: tuple(work[c, 8 + r : 9 + r, :] for c in range(8)),
                64, cells >> 7, cells & 127, [jnp.zeros((16, 128), F32)] * 8,
            )
            for i in range(2):
                for q in range(4):
                    first = got[2 * q][i * 8 : i * 8 + 8]
                    second = got[2 * q + 1][i * 8 : i * 8 + 8]
                    outbox[half, b * 2 + i, :, q, :] = jnp.where(low, first, pltpu.roll(second, 64, 1))
                    outbox[half + 2, b * 2 + i, :, q, :] = jnp.where(low, pltpu.roll(first, 64, 1), second)

        loop(0, 2, block)

    halves = (lax.rem(x + 1, 2), lax.rem(x, 2))
    order = (halves[0], halves[0] + 2, lax.rem(x + 2, 4), x)

    def round_count(from_z):
        return jnp.where(from_z == 0, 2, jnp.where(from_z < 1 + ROUND, 1, 0))

    def depart(quarter):
        to_x = order[quarter]

        def one(i):
            push(
                outbox.at[to_x, i], mid.at[to_x, z], out_send, mid_recv.at[quarter // 2], in_column((mp + 1) * ZS + i)
            )

        loop(0, ZS - round_count(z), one)

    def depart_round(t):
        def one(i):
            below = in_column(lax.rem(level + LEVELS - 7, LEVELS))
            for quarter in (2 * t, 2 * t + 1):
                push(outbox.at[order[quarter], 3 - i], relay.at[i, quarter], out_send, relay_recv.at[t], below)

        loop(0, round_count(z), one)

    relays = [
        (jnp.logical_and(mp != 1, z == 1), pl.ds(0, 2)),
        (jnp.logical_and(mp != 1, jnp.logical_and(z >= 2, z < 2 + ROUND)), pl.ds(0, 1)),
    ]

    def pass_on(t):
        for here, slots in relays:

            @pl.when(here)
            def _(slots=slots):
                wait_for(relay.at[slots, pl.ds(2 * t, 2)], relay_recv.at[t])

                def one(i):
                    to = in_column(lax.rem(mp + 3, 4) * ZS + 3 - i)
                    for quarter in (2 * t, 2 * t + 1):
                        push(relay.at[i, quarter], mid.at[order[quarter], z - 1], relay_send, mid_recv.at[t], to)

                loop(0, slots.size, one)

    pl.semaphore_wait(barrier, 8 + PLANE - 1 + 2)
    for far in (4, LEVELS - 4):
        pl.semaphore_signal(
            known, inc=1, device_id=in_column(lax.rem(level + far, LEVELS)), device_id_type=MESH
        )

    @pl.when(magnetic)
    def _():
        elsewhere_in_plane(
            lambda p: push(contribution.at[p], rs.at[place], send.at[0], recv.at[0], in_plane(p))
        )
        rs[place] = contribution[place]

    push(halo_out.at[0], halo_in.at[1], halo_send.at[0], halo_recv.at[1], before)
    push(halo_out.at[1], halo_in.at[0], halo_send.at[1], halo_recv.at[0], after)

    @pl.when(mp < 3)
    def _():
        def each(t):
            pack(lax.rem(x + 1 + t, 2))

            @pl.when(t == 0)
            def _():
                pl.semaphore_wait(known, 2)
                depart_round(0)
                depart(0)

        loop(0, 2, each)

    @pl.when(mp == 3)
    def _():
        pl.semaphore_wait(known, 2)

    @pl.when(magnetic)
    def _():
        wait_for(rs.at[pl.ds(0, PLANE - 1)], recv.at[0])
        total = rs[0]
        for i in range(1, PLANE):
            total = total + rs[i]
        part[...] = total

        for i in (8, 7, 9, 6, 10, 5, 11, 4, 12, 3, 13, 2, 14, 1, 15):
            push(part, ar.at[level - 8], send.at[1], recv.at[1], in_column(lax.rem(level + i, LEVELS)))
        ar[level - 8] = total

    loads[5].wait()
    loads[6].wait()

    @pl.when(mp > 0)
    def _():
        counts = recv_count[...]
        high = ((lane & 63) + 1).astype(F32)

        def used(b):
            return (iota((8, 128), 0) + b * 8) < counts

        slot_code[...] = invert(dst, used, lambda p: high, lambda p: ((lane >> 6) * 64 + p).astype(F32), 64).astype(I32)

    @pl.when(mp < 3)
    def _():
        depart_round(1)
        depart(1)
        depart(2)

    for i in range(2):
        wait_for(halo_in.at[i], halo_recv.at[i])
    for c in range(8):
        for i in range(2):
            work[c, 6 + i : 7 + i, :] = halo_in[0, i * 8 + c : i * 8 + c + 1, :]
            work[c, 72 + i : 73 + i, :] = halo_in[1, i * 8 + c : i * 8 + c + 1, :]
    for _ in range(2):
        sweep(work, 1, 1)
        sweep(work, 2, 0)

    @pl.when(magnetic)
    def _():
        wait_for(ar.at[pl.ds(0, 7)], recv.at[1])

    @pl.when(mp < 2)
    def _():
        wait_for(ar.at[pl.ds(0, 8)], recv.at[1])

    total = ar[0]
    for i in range(1, 8):
        total = total + ar[i]
    full[...] = total

    elsewhere_in_plane(lambda p: push(full, spread.at[place], send.at[2], recv.at[2], in_plane(p)))
    spread[place] = total

    @pl.when(mp < 3)
    def _():
        depart(3)

    pass_on(0)

    @pl.when(magnetic)
    def _():
        def used(b):
            return owner[pl.ds(b * 8, 8), :] == me

        def high(i):
            row = lax.rem(lax.div(i, 8), 4) * 32 + lax.rem(i, 2) * 16 + lax.div(i, 32) + 1
            return (row + (lane >> 5) * 4).astype(F32)

        def low(i):
            return (lax.rem(lax.div(i, 2), 4) * 32 + (lane & 31)).astype(F32)

        iono_code[...] = invert(cell, used, high, low, 128).astype(I32)

    loads[7].wait()
    wait_for(spread.at[pl.ds(0, PLANE - 1)], recv.at[2])
    acc = jnp.zeros((32, 128), F32)
    for i in range(128):
        acc = acc + response[:, i * 128 : (i + 1) * 128].astype(F32) * spread[i // 4, i % 4 : i % 4 + 1, :]
    tile[...] = jnp.zeros_like(tile)
    tile[pl.ds(pl.multiple_of(z * 32, 32), 32), :] = acc
    line[...] = jnp.sum(tile[...].T, axis=0, keepdims=True)

    def report(i):
        push(line, lines.at[level], send.at[3], recv.at[3], in_column(8 + lax.rem(level + i, 8)))

    @pl.when(magnetic)
    def _():
        loop(1, 8, report)
        lines[level] = line[...]

    @pl.when(mp < 2)
    def _():
        loop(0, 8, report)

    def forward(to_x, t, first):
        core = lax.rem(yc, 2)
        for dy in (2, 1, 3, 0):
            for dc in (0, 1):
                if first and dy + dc == 0:
                    continue
                to = lax.rem(lax.div(yc, 2) + dy, 4) * 2 + lax.rem(core + dc, 2)
                push(
                    mid.at[to_x, :, to], inbox.at[x, :, yc], fwd_send.at[t], inbox_recv.at[t], in_plane(to_x * YC + to)
                )

    pass_on(1)

    @pl.when(mp > 0)
    def _():
        wait_for(mid.at[pl.ds(0, 2)], mid_recv.at[0])
        forward(order[0], 0, 0)
        forward(order[1], 0, 0)

    @pl.when(magnetic)
    def _():
        wait_for(lines.at[pl.ds(0, LEVELS - 1)], recv.at[3])
        rows = []
        for m in range(4):
            row = lines[m * 4]
            for i in range(1, 4):
                row = row + lines[m * 4 + i]
            rows.append(row)
        mine = jnp.concatenate(rows, axis=0)
        pot_part[...] = mine

        elsewhere_in_plane(lambda p: push(pot_part, pot.at[place], send.at[4], recv.at[4], in_plane(p)))
        pot[place] = mine

    def unpack(half):
        for i in range(4):
            for q in range(4):
                first = inbox[half, i, :, q, :]
                second = inbox[half + 2, i, :, q, :]
                table[2 * q, i * 8 : i * 8 + 8, :] = jnp.where(low, first, pltpu.roll(second, 64, 1))
                table[2 * q + 1, i * 8 : i * 8 + 8, :] = jnp.where(low, pltpu.roll(first, 64, 1), second)

        def block(b):
            at = pl.ds(pl.multiple_of(8 + b * 16, 8), 16)
            row = slot_code[pl.ds(b * 16, 16), :] - (1 + half * 32)
            spot = slot_code[pl.ds(64 + b * 16, 16), :]
            got = pick(
                lambda r: tuple(table[c, r : r + 1, :] for c in range(8)),
                32, row, spot, [work[c, at, :] for c in range(8)],
            )
            for c in range(8):
                work[c, at, :] = got[c]

        loop(0, 4, block)

    @pl.when(mp > 0)
    def _():
        wait_for(mid.at[pl.ds(0, 2)], mid_recv.at[1])
        forward(order[2], 1, 0)
        forward(order[3], 1, 1)
        inbox[x, :, yc] = mid[x, :, yc]

        def each(t):
            @pl.when(t == 0)
            def _():
                wait_for(inbox.at[pl.ds(0, 2)], inbox_recv.at[0])

            @pl.when(t == 1)
            def _():
                wait_for(inbox.at[pl.ds(0, 3), :, pl.ds(0, 5)], inbox_recv.at[1])

            unpack(lax.rem(x + 1 + t, 2))

        loop(0, 2, each)

    @pl.when(magnetic)
    def _():
        wait_for(pot.at[pl.ds(0, PLANE - 1)], recv.at[4])

        def block(b):
            at = pl.ds(pl.multiple_of(8 + b * 16, 8), 16)
            row = iono_code[pl.ds(b * 16, 16), :] - 1
            spot = iono_code[pl.ds(64 + b * 16, 16), :]
            (got,) = pick(
                lambda r: (pot[r // 4, r % 4 : r % 4 + 1, :],), 128, row, spot, [jnp.zeros((16, 128), F32)]
            )
            work[1, at, :] = work[1, at, :] + 0.5 * work[0, at, :] * got

        loop(0, 4, block)

    state_out[...] = work[:, 8:72, :]

    for i in range(2):
        wait_for(halo_out.at[i], halo_send.at[i])
    wait_for(spread.at[pl.ds(0, PLANE - 1)], send.at[2])

    @pl.when(mp < 3)
    def _():
        wait_for(mid, out_send)

    for here, slots in relays:

        @pl.when(here)
        def _(slots=slots):
            wait_for(relay.at[slots], relay_send)

    @pl.when(mp > 0)
    def _():
        wait_for(inbox.at[pl.ds(0, 2)], fwd_send.at[0])
        wait_for(inbox.at[pl.ds(0, 3), :, pl.ds(0, 5)], fwd_send.at[1])

    @pl.when(magnetic)
    def _():
        wait_for(rs.at[pl.ds(0, PLANE - 1)], send.at[0])
        wait_for(ar.at[pl.ds(0, LEVELS - 1)], send.at[1])
        wait_for(lines.at[pl.ds(0, 7)], send.at[3])
        wait_for(pot.at[pl.ds(0, PLANE - 1)], send.at[4])

    @pl.when(mp < 2)
    def _():
        wait_for(lines.at[pl.ds(0, 8)], send.at[3])


def hand_out(state, density_out, fields_out, sem):
    copies = [
        pltpu.make_async_copy(state.at[0], density_out.at[0], sem.at[0]),
        pltpu.make_async_copy(state.at[pl.ds(1, 7)], fields_out.at[0], sem.at[1]),
    ]
    for copy in copies:
        copy.start()
    for copy in copies:
        copy.wait()


def local(density, fields, src_points, dst_points, recv_count, iono_owner, iono_cell, response):
    vmem = pltpu.VMEM
    dma = pltpu.SemaphoreType.DMA
    hbm = pl.BlockSpec(memory_space=pl.ANY)
    state = pl.pallas_call(
        cycle_kernel,
        out_shape=vmem((8, 64, 128), F32),
        in_specs=[hbm] * 8,
        out_specs=pl.BlockSpec(memory_space=vmem),
        scratch_shapes=[
            vmem((8, 80, 128), F32),
            vmem((64, 128), I32),
            vmem((64, 128), I32),
            vmem((1, 128), I32),
            vmem((128, 128), I32),
            vmem((128, 128), I32),
            vmem((32, 16384), BF16),
            vmem((64, 128), I32),
            vmem((64, 128), F32),
            vmem((2, 16, 128), F32),
            vmem((2, 16, 128), F32),
            vmem((4, ZS, YC, 4, 128), F32),
            vmem((4, ZS, YC, 4, 128), F32),
            vmem((4, ZS, YC, 4, 128), F32),
            vmem((2, 4, YC, 4, 128), F32),
            vmem((8, 32, 128), F32),
            vmem((PLANE, 4, 128), F32),
            vmem((PLANE, 4, 128), F32),
            vmem((4, 128), F32),
            vmem((LEVELS, 4, 128), F32),
            vmem((4, 128), F32),
            vmem((PLANE, 4, 128), F32),
            vmem((128, 128), F32),
            vmem((1, 128), F32),
            vmem((LEVELS, 1, 128), F32),
            vmem((4, 128), F32),
            vmem((PLANE, 4, 128), F32),
            vmem((128, 128), I32),
            vmem((128, 128), I32),
            dma((8,)),
            dma((2,)),
            dma((2,)),
            dma((5,)),
            dma((5,)),
            dma,
            dma((2,)),
            dma((2,)),
            dma((2,)),
            dma,
            dma((2,)),
            pltpu.SemaphoreType.REGULAR,
        ],
        compiler_params=pltpu.CompilerParams(
            collective_id=0, has_side_effects=True, vmem_limit_bytes=56 * 1024 * 1024
        ),
        name="cycle",
    )(
        density, fields, src_points[0, 0].T, dst_points[0, 0].T, recv_count[0],
        iono_owner.reshape(128, 128), iono_cell.reshape(128, 128), response,
    )
    return state[:1], state[1:][None]


def solution(mesh):
    placed = (
        P("mp", "space", None),
        P("mp", None, "space", None),
        P("mp", "space", None, None),
        P("mp", "space", None, None),
        P("mp", "space", None),
        P(),
        P(),
        P(("mp", "space"), None),
    )
    return jax.shard_map(
        local,
        mesh=mesh,
        in_specs=placed,
        out_specs=(P("mp", "space", None), P("mp", None, "space", None)),
        check_vma=False,
    )
```
